32 devices in a mesh: seq: 4 (over y, x), grp: 8 (over z, core).
Axes of the slice: x: 2, y: 2, z: 4, core: 2. Of those that a mesh axis runs over, the one named last changes fastest.
Arguments:
- p_x: bfloat16 [8, 1024, 2048], P('grp', 'seq'), may hold values from -6 to 6
- p_bc: bfloat16 [8, 1024, 256], P('grp', 'seq'), may hold values from -4 to 4
- p_dt: float32 [8, 32, 1024], P('grp', None, 'seq'), may hold values from 0.005 to 0.04
- p_decay: float32 [8, 32, 1024], P('grp', None, 'seq'), may hold values from -1 to 0
- r_x: bfloat16 [16384, 2048], P('grp', 'seq'), may hold values from -6 to 6
- r_bc: bfloat16 [16384, 256], P('grp'), may hold values from -4 to 4
- r_dt: float32 [32, 16384], P('seq', 'grp'), may hold values from 0.005 to 0.04
- r_decay: float32 [32, 16384], P('seq', 'grp'), may hold values from -1 to 0
- pack_list: int32 [8, 8], P('grp'), may hold values from -1 to 47, as said below
- resp_len: int32 [48], replicated, may hold values from 32 to 256, as said below
- resp_prompt: int32 [48], replicated, may hold values from 0 to 7, as said below
- d_skip: float32 [32], replicated, may hold values from 0.5 to 1.5
Outputs:
- p_out: bfloat16 [8, 1024, 2048], P('grp', 'seq')
- r_out: bfloat16 [16384, 2048], P('grp', 'seq')
The draws below stay inside these ranges and needn't reach their ends.
Inputs may be any that keep to these rules, and one draw needn't show every extreme that they name: `pack_list`: row g lists the responses placed on index g of grp in the order of their rows, -1 marking an empty slot; every response stands in exactly one slot. `resp_len`: a device's responses take its rows one after another from its first row in slot order; the rows after them are unused. `resp_prompt`: every prompt has exactly 6 responses.
All inputs are finite; a program needn't handle non-finite values.
Results may differ from the reference program's by a relative error of at most 0.0053.
Values may be sent and summed in bfloat16 or wider, within the bound.
A program may use at most 64 MiB of HBM per device.

```python
import math
import jax
import jax.numpy as jnp
from jax import lax

H = 32
P_SIZE = 64
N = 128
STRETCH = 256
SLOTS = 8
RPP = 6
LMAX = 256
LMIN = 32
PROMPTS = 8
PLEN = 1024
RR = 2048
RTOT = 16384
RESP = 48


def decay_rates(key, head_count):
    lowest, highest = (1e-06, 0.06)
    fraction = jax.random.uniform(jax.random.fold_in(key, 7), (head_count,), jnp.float32)
    return jnp.exp(jnp.log(lowest) + fraction * (jnp.log(highest) - jnp.log(lowest)))


def decay_values(key, salt_value, rates_per_head, output_shape, sequence_length):
    noise_key = jax.random.fold_in(key, salt_value)
    first_key, key_second, key_third = jax.random.split(noise_key, 3)
    coarse_rate = jnp.exp(jax.random.uniform(first_key, output_shape, jnp.float32, jnp.log(0.5), jnp.log(2.0)))
    flurry_groups = (jax.random.uniform(key_second, output_shape, jnp.float32) < 2.0 / sequence_length).astype(jnp.float32)
    flurry_size = jax.random.uniform(key_third, output_shape, jnp.float32, 0.22, 0.5)
    return -rates_per_head * coarse_rate - flurry_groups * flurry_size


def draw_p_decay(key, part):
    rates_per_head = decay_rates(key, H)[None, :, None]
    return decay_values(key, 11, rates_per_head, (PROMPTS, H, PLEN), PLEN)


def draw_r_decay(key, part):
    rates_per_head = decay_rates(key, H)[:, None]
    return decay_values(key, 13, rates_per_head, (H, RTOT), PLEN)


def draw_pack_list(key, part):
    slot_order = jax.random.permutation(jax.random.fold_in(key, 21), PROMPTS * SLOTS)
    slot_table = jnp.full((PROMPTS * SLOTS,), -1, jnp.int32).at[slot_order[:RESP]].set(jnp.arange(RESP, dtype=jnp.int32))
    return slot_table.reshape(PROMPTS, SLOTS)


def draw_resp_len(key, part):
    spans = jax.random.randint(jax.random.fold_in(key, 23), (RESP,), LMIN, LMAX + 1, jnp.int32)
    chosen = jax.random.randint(jax.random.fold_in(key, 29), (), 0, RESP, jnp.int32)
    return spans.at[chosen].set(LMAX).astype(jnp.int32)


def draw_resp_prompt(key, part):
    return (jax.random.permutation(jax.random.fold_in(key, 31), RESP) // RPP).astype(jnp.int32)


def block_scale(key, shape, shards, low, high):
    def one(dim, parts):
        heights = jax.random.uniform(jax.random.fold_in(jax.random.fold_in(key, 6), dim), (parts,), jnp.float32, low / len(shards), high / len(shards))
        return jnp.repeat(jnp.exp(heights), shape[dim] // parts).reshape((-1,) + (1,) * (len(shape) - dim - 1))

    level = one(*shards[0])
    for cut in shards[1:]:
        level = level * one(*cut)
    return level


def gaussian(key, extent, width, most, shards=(), held_as=jnp.bfloat16):
    level = block_scale(key, extent, shards, -0.22, 0.18) if shards else 1.0
    result = jax.random.normal(key, extent, jnp.float32) * width * level
    return jnp.minimum(jnp.maximum(result, -most), most).astype(held_as)


def setup_inputs(seed: int = 0) -> dict:
    arg_keys = jax.random.split(jax.random.key(seed), 13)
    p_x = gaussian(arg_keys[0], (PROMPTS, PLEN, H * P_SIZE), 1.0, 6.0, ((0, 8), (1, 4)))
    p_bc = gaussian(arg_keys[1], (PROMPTS, PLEN, 2 * N), (0.3 * (128 / N) ** 0.5), 4.0, ((0, 8), (1, 4)))
    p_dt = jnp.clip(jnp.exp(math.log(0.04) - 2.0794415 * jax.random.uniform(arg_keys[2], (PROMPTS, H, PLEN), jnp.float32) ** block_scale(arg_keys[2], (PROMPTS, H, PLEN), ((0, 8), (2, 4)), -0.2, 0.2)), 0.005, 0.04)
    p_decay = draw_p_decay(jax.random.fold_in(arg_keys[12], 71), 0)
    r_x = gaussian(arg_keys[4], (RTOT, H * P_SIZE), 1.0, 6.0, ((0, 8), (1, 4)))
    r_bc = gaussian(arg_keys[5], (RTOT, 2 * N), (0.3 * (128 / N) ** 0.5), 4.0, ((0, 8),))
    r_dt = jnp.clip(jnp.exp(math.log(0.04) - 2.0794415 * jax.random.uniform(arg_keys[6], (H, RTOT), jnp.float32) ** block_scale(arg_keys[6], (H, RTOT), ((0, 4), (1, 8)), -0.2, 0.2)), 0.005, 0.04)
    r_decay = draw_r_decay(jax.random.fold_in(arg_keys[12], 71), 0)
    pack_list = draw_pack_list(jax.random.fold_in(arg_keys[12], 71), 0)
    resp_len = draw_resp_len(jax.random.fold_in(arg_keys[12], 71), 0)
    resp_prompt = draw_resp_prompt(jax.random.fold_in(arg_keys[12], 71), 0)
    d_skip = jnp.clip(jax.random.uniform(arg_keys[11], (H,), jnp.float32, 0.5, 1.5), 0.5, 1.5)
    return {"p_x": p_x, "p_bc": p_bc, "p_dt": p_dt, "p_decay": p_decay, "r_x": r_x, "r_bc": r_bc, "r_dt": r_dt, "r_decay": r_decay, "pack_list": pack_list, "resp_len": resp_len, "resp_prompt": resp_prompt, "d_skip": d_skip}


def product(einsum_form, left_side, right_side):
    left_side, right_side = lax.optimization_barrier((left_side, right_side))
    return jnp.einsum(einsum_form, left_side.astype(jnp.float32), right_side.astype(jnp.float32))


def block_terms(block_x, block_bc, block_dt, block_decay, block_slot):
    length = block_x.shape[0]
    head_count = block_dt.shape[0]
    state_width = block_bc.shape[1] // 2
    inputs = block_x.reshape(length, head_count, -1)
    b_rows = block_bc[:, :state_width]
    c_rows = block_bc[:, state_width:]
    running = jnp.cumsum(block_decay, axis=1)
    before = running - block_decay
    places = jnp.arange(length)
    same_span = (block_slot[:, None] == block_slot[None, :]) & (places[None, :] <= places[:, None])
    starts_here = jnp.concatenate([jnp.ones((1,), jnp.bool_), block_slot[1:] != block_slot[:-1]])
    leader = same_span & starts_here[None, :]
    offset = jnp.sum(jnp.where(leader[None], before[:, None, :], 0.0), axis=2)
    gained = running - offset
    scores = jnp.dot(c_rows, b_rows.T, preferred_element_type=jnp.float32)
    spread = jnp.where(same_span[None], running[:, :, None] - running[:, None, :], -jnp.inf)
    mixing = (jnp.exp(spread) * block_dt[:, None, :] * scores[None]).astype(jnp.bfloat16)
    inner_part = product("hij,jhp->ihp", mixing, inputs)
    tail_rows = block_slot == block_slot[length - 1]
    to_end = jnp.where(tail_rows[None], jnp.exp(running[:, length - 1:] - running) * block_dt, 0.0)
    scaled = (to_end[:, :, None] * b_rows[None].astype(jnp.float32)).astype(jnp.bfloat16)
    local_state = product("hjn,jhp->hnp", scaled, inputs)
    return inputs, inner_part, gained, local_state, c_rows


def prompt_layer(skip_gain, whole_x, whole_bc, whole_dt, whole_decay):
    blocks = whole_x.shape[0] // STRETCH
    head_count = whole_dt.shape[0]
    state_width = whole_bc.shape[1] // 2
    sliced = (whole_x.reshape(blocks, STRETCH, -1), whole_bc.reshape(blocks, STRETCH, -1),
              whole_dt.reshape(head_count, blocks, STRETCH).transpose(1, 0, 2),
              whole_decay.reshape(head_count, blocks, STRETCH).transpose(1, 0, 2))

    def advance(carried_state, pieces):
        inputs, inner_part, gained, local_state, c_rows = block_terms(pieces[0], pieces[1], pieces[2], pieces[3], jnp.zeros((STRETCH,), jnp.int32))
        carried = product("in,hnp->ihp", c_rows, carried_state.astype(jnp.bfloat16)) * jnp.exp(gained).T[:, :, None]
        output = inner_part + carried + skip_gain[None, :, None] * inputs.astype(jnp.float32)
        carried_state = jnp.exp(gained[:, -1])[:, None, None] * carried_state + local_state
        return carried_state, output.reshape(STRETCH, -1).astype(jnp.bfloat16)

    initial = jnp.zeros((head_count, state_width, whole_x.shape[1] // head_count), jnp.float32)
    final_state, outputs = lax.scan(advance, initial, sliced)
    return outputs.reshape(whole_x.shape), final_state.astype(jnp.bfloat16)


def response_layer(skip_gain, rows_x, rows_bc, rows_dt, rows_decay, row_slot, slot_seeds):
    slot_count = slot_seeds.shape[0]
    blocks = rows_x.shape[0] // STRETCH
    head_count = rows_dt.shape[0]
    sliced = (rows_x.reshape(blocks, STRETCH, -1), rows_bc.reshape(blocks, STRETCH, -1),
              rows_dt.reshape(head_count, blocks, STRETCH).transpose(1, 0, 2),
              rows_decay.reshape(head_count, blocks, STRETCH).transpose(1, 0, 2),
              row_slot.reshape(blocks, STRETCH))
    slot_ids = jnp.arange(slot_count)

    def advance(carry_pair, pieces):
        carried_state, previous = carry_pair
        block_slot = pieces[4]
        inputs, inner_part, gained, local_state, c_rows = block_terms(pieces[0], pieces[1], pieces[2], pieces[3], block_slot)
        first_slot = block_slot[0]
        carried_on = first_slot == previous
        chosen = (slot_ids == first_slot) & carried_on
        bases_table = jnp.where(chosen[:, None, None, None], carried_state.astype(jnp.bfloat16)[None], slot_seeds)
        projected = product("in,khnp->ikhp", c_rows, bases_table)
        hot_rows = (block_slot[:, None] == slot_ids[None, :]).astype(jnp.float32)
        carried = jnp.sum(projected * hot_rows[:, :, None, None], axis=1) * jnp.exp(gained).T[:, :, None]
        output = inner_part + carried + skip_gain[None, :, None] * inputs.astype(jnp.float32)
        output = jnp.where((block_slot < slot_count)[:, None, None], output, 0.0)
        final_slot = block_slot[STRETCH - 1]
        fresh_seed = jnp.sum(jnp.where((slot_ids == final_slot)[:, None, None, None], slot_seeds.astype(jnp.float32), 0.0), axis=0)
        anchor = jnp.where((final_slot == first_slot) & carried_on, carried_state, fresh_seed)
        carried_state = jnp.exp(gained[:, -1])[:, None, None] * anchor + local_state
        return (carried_state, final_slot), output.reshape(STRETCH, -1).astype(jnp.bfloat16)

    initial = (jnp.zeros(slot_seeds.shape[1:], jnp.float32), jnp.int32(-1))
    final_pair, outputs = lax.scan(advance, initial, sliced)
    return outputs.reshape(rows_x.shape)


def slot_layout(pack_row, resp_len, resp_prompt, row_count):
    hit_table = pack_row[:, None] == jnp.arange(resp_len.shape[0])[None, :]
    slot_spans = jnp.sum(jnp.where(hit_table, resp_len[None, :], 0), axis=1).astype(jnp.int32)
    owners = jnp.where(pack_row >= 0, jnp.sum(jnp.where(hit_table, resp_prompt[None, :], 0), axis=1), -1)
    limits = jnp.cumsum(slot_spans)
    row_slot = jnp.sum((jnp.arange(row_count)[:, None] >= limits[None, :]).astype(jnp.int32), axis=1)
    return row_slot.astype(jnp.int32), owners.astype(jnp.int32)


def reference(p_x, p_bc, p_dt, p_decay, r_x, r_bc, r_dt, r_decay, pack_list, resp_len, resp_prompt, d_skip):
    def one_prompt(element):
        return prompt_layer(d_skip, element[0], element[1], element[2], element[3])

    p_out, seeds_all = lax.map(one_prompt, (p_x, p_bc, p_dt, p_decay))
    head_count = r_dt.shape[0]
    rows_dt = r_dt.reshape(head_count, PROMPTS, RR).transpose(1, 0, 2)
    rows_decay = r_decay.reshape(head_count, PROMPTS, RR).transpose(1, 0, 2)

    def one_device(element):
        row_slot, owners = slot_layout(element[4], resp_len, resp_prompt, RR)
        pick_table = (owners[:, None] == jnp.arange(PROMPTS)[None, :]).astype(jnp.float32)
        slot_seeds = product("kq,qhnp->khnp", pick_table, seeds_all).astype(jnp.bfloat16)
        return response_layer(d_skip, element[0], element[1], element[2], element[3], row_slot, slot_seeds)

    r_out = lax.map(one_device, (r_x.reshape(PROMPTS, RR, -1), r_bc.reshape(PROMPTS, RR, -1), rows_dt, rows_decay, pack_list))
    return p_out, r_out.reshape(r_x.shape)
```

```python
import functools

import jax
import jax.numpy as jnp
from jax import lax
from jax.experimental import pallas as pl
from jax.experimental.pallas import tpu as pltpu
from jax.sharding import PartitionSpec as P

TILE = 128
STATE = 128
CHANNELS = 64
LOG2E = 1.4426950408889634
F32 = jnp.float32
BF16 = jnp.bfloat16
MESH = pl.DeviceIdType.MESH


def dot(a, b):
    return jnp.dot(a, b, preferred_element_type=F32)


def dot_nt(a, b):
    return lax.dot_general(a, b, (((1,), (1,)), ((), ())), preferred_element_type=F32)


def dot_tn(a, b):
    return lax.dot_general(a, b, (((0,), (0,)), ((), ())), preferred_element_type=F32)


def split(value, terms):
    parts = []
    for _ in range(terms):
        part = value.astype(BF16).astype(F32)
        parts.append(part)
        value = value - part
    return parts


def iota(shape, dim):
    return lax.broadcasted_iota(jnp.int32, shape, dim)


def spreader(rows, columns, bases):
    row = iota((rows, columns), 0)
    head = iota((rows, columns), 1) >> 6
    hit = row == head + bases[0]
    for base in bases[1:]:
        hit = hit | (row == head + base)
    return jnp.where(hit, 1.0, 0.0).astype(BF16)


def paired(x_pair):
    first = iota(x_pair.shape, 1) < CHANNELS
    wide = x_pair.astype(F32)
    return jnp.concatenate([jnp.where(first, wide, 0.0), jnp.where(first, 0.0, wide)], axis=0).astype(BF16)


def diagonal(column, row, bias, scores, x_tile, heads):
    pieces = []
    for pair in range(heads // 2):
        mixes = []
        for h in (2 * pair, 2 * pair + 1):
            power = column[:, h : h + 1] + (row[h : h + 1, :] + bias)
            mixes.append((jnp.exp2(power) * scores).astype(BF16))
        x_pair = x_tile[:, pair * 2 * CHANNELS : (pair + 1) * 2 * CHANNELS]
        pieces.append(dot(jnp.concatenate(mixes, axis=1), paired(x_pair)))
    return pieces


def kernel(
    sizes,
    px_hbm, pbc_hbm, pdt_ref, pdec_ref, rx_hbm, rbc_hbm, rdt_ref, rdec_ref, pack_ref, len_ref, prm_ref, d_ref,
    pout_hbm, rout_hbm,
    px, pbc, rx, rbc, pv, pt, pe, ptot, pacc, dwide, rv, rt, re, rtot, racc, rdecs,
    abuf, arecv, pbuf, precv, seeds, pout, rout,
    in_sem, out_sem, a_send, a_recv, x_send, x_recv, g_recv, up_send, down_send, tu_send, td_send,
):
    seqs, grps, heads, block_heads, head_rows, slots, tiles = sizes
    cols = heads * CHANNELS
    cb = block_heads * CHANNELS
    me = lax.axis_index("seq")
    g = lax.axis_index("grp")
    z, core = g // 2, lax.rem(g, 2)
    levels = grps // 2
    twin = z * 2 + 1 - core

    loads = [
        pltpu.make_async_copy(px_hbm, px, in_sem.at[0]),
        pltpu.make_async_copy(pbc_hbm, pbc, in_sem.at[1]),
        pltpu.make_async_copy(rx_hbm, rx, in_sem.at[2]),
        pltpu.make_async_copy(rbc_hbm, rbc.at[pl.ds(2 * TILE, tiles * TILE)], in_sem.at[3]),
    ]
    for load in loads:
        load.start()

    barrier = pltpu.get_barrier_semaphore()
    for step in range(1, seqs):
        pl.semaphore_signal(barrier, inc=1, device_id={"seq": lax.rem(me + step, seqs)}, device_id_type=MESH)
    pl.semaphore_signal(barrier, inc=1, device_id={"grp": twin}, device_id_type=MESH)

    @pl.when(z > 0)
    def _():
        pl.semaphore_signal(barrier, inc=1, device_id={"grp": g - 2}, device_id_type=MESH)

    @pl.when(z < levels - 1)
    def _():
        pl.semaphore_signal(barrier, inc=1, device_id={"grp": g + 2}, device_id_type=MESH)

    pe[0] = spreader(TILE, cols, (32, 64))
    pe[1] = spreader(TILE, cols, (0, 32))
    re[0] = spreader(TILE, cb, (head_rows, 2 * head_rows))
    re[1] = spreader(TILE, cb, (3 * head_rows, 4 * head_rows))
    re[2] = spreader(TILE, cb, (5 * head_rows, 6 * head_rows))
    row8 = iota((8, heads), 0)
    skips = split(jnp.broadcast_to(d_ref[...], (8, heads)), 3)
    skip_rows = jnp.where(row8 == 0, skips[0], jnp.where(row8 == 1, skips[1], jnp.where(row8 == 2, skips[2], 0.0)))
    skip_wide = dot(skip_rows.astype(BF16), spreader(heads, cols, (0,)))
    dwide[...] = jnp.broadcast_to(jnp.sum(skip_wide, axis=0, keepdims=True), (8, cols))

    before = iota((TILE, TILE), 0) <= iota((TILE, TILE), 1)
    upper = jnp.where(before, 1.0, 0.0).astype(BF16)
    low_bias = jnp.where(iota((TILE, TILE), 1) <= iota((TILE, TILE), 0), 0.0, -1e30)

    prow = []
    for t in range(2):
        lanes = slice(t * TILE, (t + 1) * TILE)
        parts = split(pdec_ref[:, lanes], 3)
        sums = dot(jnp.concatenate(parts, axis=0).astype(BF16), upper)
        cum = sums[:heads] + sums[heads : 2 * heads] + sums[2 * heads :]
        dt = pdt_ref[:, lanes]
        c2 = cum * LOG2E
        prow.append(jnp.log2(dt) - c2)
        grown = split(jnp.exp2(c2), 2)
        weight = split(jnp.exp2(c2[:, TILE - 1 :] - c2) * dt, 2)
        fill = jnp.zeros((TILE - 3 * heads, TILE), F32)
        pt[2 * t] = jnp.concatenate([c2] + grown + [fill], axis=0).T
        fill = jnp.zeros((TILE - 2 * heads, TILE), F32)
        pt[2 * t + 1] = jnp.concatenate(weight + [fill], axis=0).T
    loads[0].wait()
    loads[1].wait()
    chunk = min(cols, 512)
    for t in range(2):
        rows = slice(t * TILE, (t + 1) * TILE)
        for start in range(0, cols, chunk):
            here = slice(start, start + chunk)
            wide = dot(pt[2 * t + 1].astype(BF16), pe[1, :, here])
            pv[t, :, here] = (px[rows, here].astype(F32) * wide).astype(BF16)
            last = dot(pt[2 * t, TILE - 8 :, :].astype(BF16), pe[0, :, here])
            ptot[t, :, here] = jnp.broadcast_to(last[7:8], (8, chunk))
    for s in range(seqs):
        here = slice(s * cb, (s + 1) * cb)
        t0, t1 = ptot[0, 0:1, here], ptot[1, 0:1, here]
        ended = t1 * dot_tn(pbc[0:TILE, :STATE], pv[0, :, here]) + dot_tn(pbc[TILE:, :STATE], pv[1, :, here])
        abuf[s, 0:STATE, :] = ended.astype(BF16)
        hi, lo = split(t0 * t1, 2)
        row = iota((16, cb), 0)
        abuf[s, STATE:, :] = jnp.where(row == 0, hi, jnp.where(row == 1, lo, 0.0)).astype(BF16)

    pl.semaphore_wait(barrier, seqs + jnp.where(z > 0, 1, 0) + jnp.where(z < levels - 1, 1, 0))

    def state_copy(step):
        peer = lax.rem(me + step, seqs)
        return pltpu.make_async_remote_copy(
            src_ref=abuf.at[peer], dst_ref=arecv.at[me], send_sem=a_send.at[step], recv_sem=a_recv.at[step],
            device_id={"seq": peer}, device_id_type=MESH)

    def prefix_copy(step):
        peer = lax.rem(me + step, seqs)
        return peer, pltpu.make_async_remote_copy(
            src_ref=pbuf.at[peer], dst_ref=precv.at[me], send_sem=x_send.at[step], recv_sem=x_recv.at[step],
            device_id={"seq": peer}, device_id_type=MESH)

    def seed_copy(level, target, send_sem):
        which = level * 2 + core
        return pltpu.make_async_remote_copy(
            src_ref=seeds.at[which], dst_ref=seeds.at[which], send_sem=send_sem, recv_sem=g_recv.at[which],
            device_id={"grp": target}, device_id_type=MESH)

    for step in range(1, seqs):
        state_copy(step).start()
    arecv[me] = abuf[me]

    for t in range(2):
        rows = slice(t * TILE, (t + 1) * TILE)
        b_rows, c_rows = pbc[rows, :STATE], pbc[rows, STATE:]
        scores = dot_nt(c_rows, b_rows)
        column = pt[2 * t]
        x_tile = px[rows, :]
        pieces = diagonal(column, prow[t], low_bias, scores, x_tile, heads)
        for pair, piece in enumerate(pieces):
            here = slice(pair * 2 * CHANNELS, (pair + 1) * 2 * CHANNELS)
            pacc[rows, here] = piece + dwide[0:1, here] * x_tile[:, here].astype(F32)
        if t == 1:
            cross = dot_nt(c_rows, pbc[0:TILE, :STATE]).astype(BF16)
            for start in range(0, cols, chunk):
                here = slice(start, start + chunk)
                grown = dot(column.astype(BF16), pe[0, :, here])
                pacc[rows, here] += grown * dot(cross, pv[0, :, here])

    limits, owners, edge = [], [], jnp.int32(0)
    for k in range(slots):
        which = pack_ref[0, k]
        there = which >= 0
        which = jnp.maximum(which, 0)
        owners.append(jnp.where(there, prm_ref[which], -1))
        limits.append(edge)
        edge = edge + jnp.where(there, len_ref[which], 0)
    limits.append(edge)

    rbc[0 : 2 * TILE, :] = jnp.zeros((2 * TILE, 2 * STATE), BF16)
    rv[0:2] = jnp.zeros((2, TILE, cb), BF16)
    rtot[0:2] = jnp.zeros((2, 8, cb), F32)
    parts = split(rdec_ref[...], 3)
    rdecs[:, 0 : 2 * TILE] = jnp.zeros((4 * head_rows, 2 * TILE), BF16)
    rdecs[:, 2 * TILE :] = jnp.concatenate(parts + [jnp.zeros_like(parts[0])], axis=0).astype(BF16)
    my_cols = pl.ds(pl.multiple_of(me * cb, cb), cb)
    loads[2].wait()
    loads[3].wait()

    def response_tile(tile, carry):
        base = pl.multiple_of(tile * TILE, TILE)
        rows = pl.ds(base, TILE)
        place = base + iota((8, TILE), 1)
        start = jnp.zeros((8, TILE), jnp.int32)
        owner = jnp.full((8, TILE), -1, jnp.int32)
        for k in range(slots):
            start = jnp.where(place >= limits[k], limits[k], start)
            owner = jnp.where((place >= limits[k]) & (place < limits[k + 1]), owners[k], owner)
        start = jnp.where(place >= limits[slots], limits[slots], start) - base

        j = iota((3 * TILE, TILE), 0) - 2 * TILE
        i = iota((3 * TILE, TILE), 1)
        ordered = j <= i
        in_slot = jnp.where(ordered & (j >= start[0:1]), 1.0, 0.0)
        in_tile = jnp.where(ordered & (j >= 0), 1.0, 0.0)
        sums = dot(rdecs[:, pl.ds(base, 3 * TILE)], jnp.concatenate([in_slot, in_tile], axis=1).astype(BF16))
        sums = sums[:head_rows] + sums[head_rows : 2 * head_rows] + sums[2 * head_rows : 3 * head_rows]
        gain, c2 = sums[:, :TILE] * LOG2E, sums[:, TILE:] * LOG2E
        dt = rdt_ref[:, rows]
        row_form = jnp.log2(dt) - c2
        where_rows = jnp.where(iota((8, TILE), 0) == 0, start, owner).astype(F32)
        stack = [c2] + split(jnp.exp2(c2), 2) + split(jnp.exp2(c2[:, TILE - 1 :] - c2) * dt, 2)
        stack += split(jnp.exp2(gain), 2) + [where_rows]
        stack += [jnp.zeros((TILE - 7 * head_rows - 8, TILE), F32)]
        column = jnp.concatenate(stack, axis=0).T
        rt[tile] = column
        narrow = column.astype(BF16)

        x_tile = rx[rows, :]
        wide = dot(narrow, re[1])
        rv[tile + 2] = (x_tile.astype(F32) * wide).astype(BF16)
        grown = dot(narrow, re[0])
        rtot[tile + 2] = jnp.broadcast_to(grown[TILE - 1 :], (8, cb))

        c_rows = rbc[pl.ds(base + 2 * TILE, TILE), STATE:]
        scores = dot_nt(c_rows, rbc[pl.ds(base, 3 * TILE), :STATE])
        j = iota((TILE, 3 * TILE), 1) - 2 * TILE
        first = column[:, 7 * head_rows : 7 * head_rows + 1].astype(jnp.int32)
        seen = (j <= iota((TILE, 3 * TILE), 0)) & (j >= first)
        bias = jnp.where(seen[:, 2 * TILE :], 0.0, -1e30)
        cross = jnp.where(seen[:, : 2 * TILE], scores[:, : 2 * TILE], 0.0).astype(BF16)
        earlier = dot(cross[:, TILE:], rv[tile + 1]) + rtot[tile + 1, 0:1] * dot(cross[:, :TILE], rv[tile])
        pieces = diagonal(column, row_form, bias, scores[:, 2 * TILE :], x_tile, block_heads)
        skip = dwide[0:1, my_cols]
        racc[rows, :] = jnp.concatenate(pieces, axis=1) + grown * earlier + skip * x_tile.astype(F32)
        return carry

    share = tiles // 4
    lax.fori_loop(0, share, response_tile, 0)

    for step in range(1, seqs):
        state_copy(step).wait_recv()
    ahead = jnp.zeros((STATE, cb), F32)
    for s in range(seqs):
        pbuf[s] = ahead.astype(BF16)
        decay = arecv[s, STATE:, :].astype(F32)
        ahead = (decay[0:1] + decay[1:2]) * ahead + arecv[s, 0:STATE, :].astype(F32)
    seeds[g] = ahead.astype(BF16)

    def pass_on(level, distance, up):
        if up:
            @pl.when(z < levels - 1)
            def _():
                seed_copy(level, g + 2, up_send.at[distance]).start()
        else:
            @pl.when(z > 0)
            def _():
                seed_copy(level, g - 2, down_send.at[distance]).start()

    pass_on(z, 0, True)
    pass_on(z, 0, False)
    seed_copy(z, twin, tu_send.at[0]).start()
    for step in range(1, seqs):
        peer, copy = prefix_copy(step)

        @pl.when(peer > 0)
        def _():
            copy.start()

    precv[me] = pbuf[me]

    def relay(distance):
        @pl.when(z >= distance)
        def _():
            seed_copy(z - distance, twin, tu_send.at[distance]).wait_recv()
            pass_on(z - distance, distance, True)
            seed_copy(z - distance, twin, tu_send.at[distance]).start()

        @pl.when(z + distance < levels)
        def _():
            seed_copy(z + distance, twin, td_send.at[distance]).wait_recv()
            pass_on(z + distance, distance, False)
            seed_copy(z + distance, twin, td_send.at[distance]).start()

    lax.fori_loop(share, 2 * share, response_tile, 0)
    relay(1)
    lax.fori_loop(2 * share, 3 * share, response_tile, 0)
    if levels > 2:
        relay(2)
    lax.fori_loop(3 * share, tiles, response_tile, 0)

    for step in range(1, seqs):
        copy = prefix_copy(step)[1]

        @pl.when(me > 0)
        def _():
            copy.wait_recv()

    @pl.when(me == 0)
    def _():
        for s in range(seqs):
            precv[s] = jnp.zeros((STATE, cb), BF16)

    p_outs = []
    for t in range(2):
        rows = slice(t * TILE, (t + 1) * TILE)
        narrow = pt[2 * t].astype(BF16)
        for s in range(seqs):
            here = slice(s * cb, (s + 1) * cb)
            grown = dot(narrow, pe[0, :, here])
            if t == 1:
                grown = grown * ptot[0, 0:1, here]
            carried = grown * dot(pbc[rows, STATE:], precv[s])
            pout[rows, here] = (pacc[rows, here] + carried).astype(BF16)
        p_outs.append(pltpu.make_async_copy(pout.at[rows], pout_hbm.at[rows], out_sem.at[tiles + t]))
        p_outs[-1].start()

    for distance in range(3, levels):
        relay(distance)
    for level in range(levels):
        which = level * 2 + 1 - core
        pltpu.make_async_remote_copy(
            src_ref=seeds.at[which], dst_ref=seeds.at[which], send_sem=tu_send.at[0], recv_sem=g_recv.at[which],
            device_id={"grp": twin}, device_id_type=MESH).wait_recv()

    def out_copy(tile):
        rows = pl.ds(pl.multiple_of(tile * TILE, TILE), TILE)
        return pltpu.make_async_copy(rout.at[rows], rout_hbm.at[rows], out_sem.at[tile])

    def seed_tile(tile, carry):
        base = pl.multiple_of(tile * TILE, TILE)
        rows = pl.ds(base, TILE)
        column = rt[tile]
        owner = column[:, 7 * head_rows + 1 : 7 * head_rows + 2].astype(jnp.int32)
        c_rows = rbc[pl.ds(base + 2 * TILE, TILE), STATE:].astype(F32)
        batch = 8 if grps % 8 == 0 else 2
        total = jnp.zeros((TILE, cb), F32)
        for q in range(0, grps, batch):
            chosen = [jnp.where(owner == q + n, c_rows, 0.0) for n in range(batch)]
            table = seeds[q : q + batch].reshape(batch * STATE, cb)
            total = total + dot(jnp.concatenate(chosen, axis=1).astype(BF16), table)
        result = racc[rows, :] + dot(column.astype(BF16), re[2]) * total
        rout[rows, :] = jnp.where(owner >= 0, result, 0.0).astype(BF16)
        out_copy(tile).start()
        return carry

    lax.fori_loop(0, tiles, seed_tile, 0)

    for step in range(1, seqs):
        state_copy(step).wait_send()
        peer, copy = prefix_copy(step)

        @pl.when(peer > 0)
        def _():
            copy.wait_send()

    for distance in range(levels):
        @pl.when((z >= distance) & (z < levels - 1))
        def _():
            seed_copy(z - distance, g + 2, up_send.at[distance]).wait_send()

        @pl.when((z + distance < levels) & (z > 0))
        def _():
            seed_copy(z + distance, g - 2, down_send.at[distance]).wait_send()

        @pl.when(z >= distance)
        def _():
            seed_copy(z - distance, twin, tu_send.at[distance]).wait_send()

        if distance > 0:
            @pl.when(z + distance < levels)
            def _():
                seed_copy(z + distance, twin, td_send.at[distance]).wait_send()

    for copy in p_outs:
        copy.wait()

    def out_wait(tile, carry):
        out_copy(tile).wait()
        return carry

    lax.fori_loop(0, tiles, out_wait, 0)


def on_device(
    p_x, p_bc, p_dt, p_decay, r_x, r_bc, r_dt, r_decay, pack_list, resp_len, resp_prompt, d_skip
):
    seqs, grps = lax.axis_size("seq"), lax.axis_size("grp")
    heads = p_dt.shape[1]
    block_heads = heads // seqs
    head_rows = max(8, block_heads)
    slots = pack_list.shape[1]
    tiles = r_x.shape[0] // TILE
    cols, cb = heads * CHANNELS, block_heads * CHANNELS
    if head_rows > block_heads:
        extra = ((0, head_rows - block_heads), (0, 0))
        r_dt, r_decay = jnp.pad(r_dt, extra, constant_values=1.0), jnp.pad(r_decay, extra)
    sizes = (seqs, grps, heads, block_heads, head_rows, slots, tiles)
    levels = grps // 2
    anywhere = pl.BlockSpec(memory_space=pl.ANY)
    vmem = pl.BlockSpec(memory_space=pltpu.VMEM)
    smem = pl.BlockSpec(memory_space=pltpu.SMEM)
    dma = pltpu.SemaphoreType.DMA
    p_out, r_out = pl.pallas_call(
        functools.partial(kernel, sizes),
        out_shape=(
            jax.ShapeDtypeStruct((2 * TILE, cols), BF16),
            jax.ShapeDtypeStruct((tiles * TILE, cb), BF16),
        ),
        in_specs=[anywhere, anywhere, vmem, vmem, anywhere, anywhere, vmem, vmem, smem, smem, smem, vmem],
        out_specs=(anywhere, anywhere),
        scratch_shapes=[
            pltpu.VMEM((2 * TILE, cols), BF16),
            pltpu.VMEM((2 * TILE, 2 * STATE), BF16),
            pltpu.VMEM((tiles * TILE, cb), BF16),
            pltpu.VMEM(((tiles + 2) * TILE, 2 * STATE), BF16),
            pltpu.VMEM((2, TILE, cols), BF16),
            pltpu.VMEM((4, TILE, TILE), F32),
            pltpu.VMEM((2, TILE, cols), BF16),
            pltpu.VMEM((2, 8, cols), F32),
            pltpu.VMEM((2 * TILE, cols), F32),
            pltpu.VMEM((8, cols), F32),
            pltpu.VMEM((tiles + 2, TILE, cb), BF16),
            pltpu.VMEM((tiles, TILE, TILE), F32),
            pltpu.VMEM((3, TILE, cb), BF16),
            pltpu.VMEM((tiles + 2, 8, cb), F32),
            pltpu.VMEM((tiles * TILE, cb), F32),
            pltpu.VMEM((4 * head_rows, (tiles + 2) * TILE), BF16),
            pltpu.VMEM((seqs, STATE + 16, cb), BF16),
            pltpu.VMEM((seqs, STATE + 16, cb), BF16),
            pltpu.VMEM((seqs, STATE, cb), BF16),
            pltpu.VMEM((seqs, STATE, cb), BF16),
            pltpu.VMEM((grps, STATE, cb), BF16),
            pltpu.VMEM((2 * TILE, cols), BF16),
            pltpu.VMEM((tiles * TILE, cb), BF16),
            dma((4,)),
            dma((tiles + 2,)),
            dma((seqs,)),
            dma((seqs,)),
            dma((seqs,)),
            dma((seqs,)),
            dma((grps,)),
            dma((levels,)),
            dma((levels,)),
            dma((levels,)),
            dma((levels,)),
        ],
        compiler_params=pltpu.CompilerParams(
            collective_id=0, has_side_effects=True, vmem_limit_bytes=48 * 2**20
        ),
        cost_estimate=pl.CostEstimate(flops=4 * 10**9, bytes_accessed=8 * 10**6, transcendentals=4 * 10**6),
        name="scan_and_seeds",
    )(
        p_x[0], p_bc[0], p_dt[0], p_decay[0], r_x, r_bc, r_dt, r_decay,
        pack_list, resp_len, resp_prompt, d_skip[None],
    )
    return p_out[None], r_out


def solution(mesh):
    placed = (
        P("grp", "seq", None),
        P("grp", "seq", None),
        P("grp", None, "seq"),
        P("grp", None, "seq"),
        P("grp", "seq"),
        P("grp", None),
        P("seq", "grp"),
        P("seq", "grp"),
        P("grp", None),
        P(),
        P(),
        P(),
    )
    return jax.shard_map(
        on_device,
        mesh=mesh,
        in_specs=placed,
        out_specs=(P("grp", "seq", None), P("grp", "seq")),
        check_vma=False,
    )
```

```python
import functools

import jax
import jax.numpy as jnp
from jax import lax
from jax.experimental import pallas as pl
from jax.experimental.pallas import tpu as pltpu
from jax.sharding import PartitionSpec as P

TILE = 128
STATE = 128
CHANNELS = 64
LOG2E = 1.4426950408889634
F32 = jnp.float32
BF16 = jnp.bfloat16
MESH = pl.DeviceIdType.MESH


def dot(a, b):
    return jnp.dot(a, b, preferred_element_type=F32)


def dot_nt(a, b):
    return lax.dot_general(a, b, (((1,), (1,)), ((), ())), preferred_element_type=F32)


def dot_tn(a, b):
    return lax.dot_general(a, b, (((0,), (0,)), ((), ())), preferred_element_type=F32)


def split(value, terms):
    parts = []
    for _ in range(terms):
        part = value.astype(BF16).astype(F32)
        parts.append(part)
        value = value - part
    return parts


def iota(shape, dim):
    return lax.broadcasted_iota(jnp.int32, shape, dim)


def spreader(rows, columns, bases):
    row = iota((rows, columns), 0)
    head = iota((rows, columns), 1) >> 6
    hit = row == head + bases[0]
    for base in bases[1:]:
        hit = hit | (row == head + base)
    return jnp.where(hit, 1.0, 0.0).astype(BF16)


def paired(x_pair):
    first = iota(x_pair.shape, 1) < CHANNELS
    wide = x_pair.astype(F32)
    return jnp.concatenate([jnp.where(first, wide, 0.0), jnp.where(first, 0.0, wide)], axis=0).astype(BF16)


def diagonal(column, row, bias, scores, x_tile, heads):
    pieces = []
    for pair in range(heads // 2):
        mixes = []
        for h in (2 * pair, 2 * pair + 1):
            power = column[:, h : h + 1] + (row[h : h + 1, :] + bias)
            mixes.append((jnp.exp2(power) * scores).astype(BF16))
        x_pair = x_tile[:, pair * 2 * CHANNELS : (pair + 1) * 2 * CHANNELS]
        pieces.append(dot(jnp.concatenate(mixes, axis=1), paired(x_pair)))
    return pieces


def kernel(
    sizes,
    px_hbm, pbc_hbm, pdt_hbm, pdec_hbm, rx_hbm, rbc_hbm, rdt_hbm, rdec_hbm, pack_hbm, len_hbm, prm_hbm, d_hbm,
    pout_hbm, rout_hbm,
    pdt_ref, pdec_ref, rdt, rdec_ref, pack_ref, len_ref, prm_ref, d_ref, rrow,
    px, pbc, rx, rbc, pv, pt, pe, ptot, pacc, dwide, rv, rt, re, rtot, racc, rdecs,
    abuf, arecv, pbuf, precv, seeds, pout, rout,
    in_sem, out_sem, a_send, a_recv, x_send, x_recv, g_recv, up_send, down_send, tu_send, td_send,
):
    seqs, grps, heads, block_heads, head_rows, slots, tiles = sizes
    cols = heads * CHANNELS
    cb = block_heads * CHANNELS
    me = lax.axis_index("seq")
    g = lax.axis_index("grp")
    z, core = g // 2, lax.rem(g, 2)
    levels = grps // 2
    twin = z * 2 + 1 - core

    loads = [
        pltpu.make_async_copy(px_hbm, px, in_sem.at[0]),
        pltpu.make_async_copy(pbc_hbm, pbc, in_sem.at[1]),
        pltpu.make_async_copy(rx_hbm, rx, in_sem.at[2]),
        pltpu.make_async_copy(rbc_hbm, rbc.at[pl.ds(2 * TILE, tiles * TILE)], in_sem.at[3]),
    ]
    small = [(pdec_hbm, pdec_ref), (pdt_hbm, pdt_ref), (d_hbm, d_ref), (pack_hbm, pack_ref), (len_hbm, len_ref),
             (prm_hbm, prm_ref), (rdec_hbm, rdec_ref), (rdt_hbm, rdt)]
    loads += [pltpu.make_async_copy(src, dst, in_sem.at[4 + n]) for n, (src, dst) in enumerate(small)]
    for n in (4, 5, 0, 1, 6, 7, 8, 9, 10, 11, 2, 3):
        loads[n].start()

    barrier = pltpu.get_barrier_semaphore()
    for step in range(1, seqs):
        pl.semaphore_signal(barrier, inc=1, device_id={"seq": lax.rem(me + step, seqs)}, device_id_type=MESH)
    pl.semaphore_signal(barrier, inc=1, device_id={"grp": twin}, device_id_type=MESH)

    @pl.when(z > 0)
    def _():
        pl.semaphore_signal(barrier, inc=1, device_id={"grp": g - 2}, device_id_type=MESH)

    @pl.when(z < levels - 1)
    def _():
        pl.semaphore_signal(barrier, inc=1, device_id={"grp": g + 2}, device_id_type=MESH)

    pe[0] = spreader(TILE, cols, (32, 64))
    pe[1] = spreader(TILE, cols, (0, 32))
    re[0] = spreader(TILE, cb, (head_rows, 2 * head_rows))
    re[1] = spreader(TILE, cb, (3 * head_rows, 4 * head_rows))
    re[2] = spreader(TILE, cb, (5 * head_rows, 6 * head_rows))
    for n in (4, 5, 6):
        loads[n].wait()
    row8 = iota((8, heads), 0)
    skips = split(jnp.broadcast_to(d_ref[...], (8, heads)), 3)
    skip_rows = jnp.where(row8 == 0, skips[0], jnp.where(row8 == 1, skips[1], jnp.where(row8 == 2, skips[2], 0.0)))
    skip_wide = dot(skip_rows.astype(BF16), spreader(heads, cols, (0,)))
    dwide[...] = jnp.broadcast_to(jnp.sum(skip_wide, axis=0, keepdims=True), (8, cols))

    before = iota((TILE, TILE), 0) <= iota((TILE, TILE), 1)
    upper = jnp.where(before, 1.0, 0.0).astype(BF16)
    low_bias = jnp.where(iota((TILE, TILE), 1) <= iota((TILE, TILE), 0), 0.0, -1e30)

    prow = []
    for t in range(2):
        lanes = slice(t * TILE, (t + 1) * TILE)
        parts = split(pdec_ref[:, lanes], 3)
        sums = dot(jnp.concatenate(parts, axis=0).astype(BF16), upper)
        cum = sums[:heads] + sums[heads : 2 * heads] + sums[2 * heads :]
        dt = pdt_ref[:, lanes]
        c2 = cum * LOG2E
        prow.append(jnp.log2(dt) - c2)
        grown = split(jnp.exp2(c2), 2)
        weight = split(jnp.exp2(c2[:, TILE - 1 :] - c2) * dt, 2)
        fill = jnp.zeros((TILE - 3 * heads, TILE), F32)
        pt[2 * t] = jnp.concatenate([c2] + grown + [fill], axis=0).T
        fill = jnp.zeros((TILE - 2 * heads, TILE), F32)
        pt[2 * t + 1] = jnp.concatenate(weight + [fill], axis=0).T
    loads[0].wait()
    loads[1].wait()
    chunk = min(cols, 512)
    for t in range(2):
        rows = slice(t * TILE, (t + 1) * TILE)
        for start in range(0, cols, chunk):
            here = slice(start, start + chunk)
            wide = dot(pt[2 * t + 1].astype(BF16), pe[1, :, here])
            pv[t, :, here] = (px[rows, here].astype(F32) * wide).astype(BF16)
            last = dot(pt[2 * t, TILE - 8 :, :].astype(BF16), pe[0, :, here])
            ptot[t, :, here] = jnp.broadcast_to(last[7:8], (8, chunk))
    for s in range(seqs):
        here = slice(s * cb, (s + 1) * cb)
        t0, t1 = ptot[0, 0:1, here], ptot[1, 0:1, here]
        ended = t1 * dot_tn(pbc[0:TILE, :STATE], pv[0, :, here]) + dot_tn(pbc[TILE:, :STATE], pv[1, :, here])
        abuf[s, 0:STATE, :] = ended.astype(BF16)
        hi, lo = split(t0 * t1, 2)
        row = iota((16, cb), 0)
        abuf[s, STATE:, :] = jnp.where(row == 0, hi, jnp.where(row == 1, lo, 0.0)).astype(BF16)

    pl.semaphore_wait(barrier, seqs + jnp.where(z > 0, 1, 0) + jnp.where(z < levels - 1, 1, 0))

    def state_copy(step):
        peer = lax.rem(me + step, seqs)
        return pltpu.make_async_remote_copy(
            src_ref=abuf.at[peer], dst_ref=arecv.at[me], send_sem=a_send.at[step], recv_sem=a_recv.at[step],
            device_id={"seq": peer}, device_id_type=MESH)

    def prefix_copy(step):
        peer = lax.rem(me + step, seqs)
        return peer, pltpu.make_async_remote_copy(
            src_ref=pbuf.at[peer], dst_ref=precv.at[me], send_sem=x_send.at[step], recv_sem=x_recv.at[step],
            device_id={"seq": peer}, device_id_type=MESH)

    def seed_copy(level, target, send_sem):
        which = level * 2 + core
        return pltpu.make_async_remote_copy(
            src_ref=seeds.at[which], dst_ref=seeds.at[which], send_sem=send_sem, recv_sem=g_recv.at[which],
            device_id={"grp": target}, device_id_type=MESH)

    for step in range(1, seqs):
        state_copy(step).start()
    arecv[me] = abuf[me]

    for t in range(2):
        rows = slice(t * TILE, (t + 1) * TILE)
        b_rows, c_rows = pbc[rows, :STATE], pbc[rows, STATE:]
        scores = dot_nt(c_rows, b_rows)
        column = pt[2 * t]
        x_tile = px[rows, :]
        pieces = diagonal(column, prow[t], low_bias, scores, x_tile, heads)
        for pair, piece in enumerate(pieces):
            here = slice(pair * 2 * CHANNELS, (pair + 1) * 2 * CHANNELS)
            pacc[rows, here] = piece + dwide[0:1, here] * x_tile[:, here].astype(F32)
        if t == 1:
            cross = dot_nt(c_rows, pbc[0:TILE, :STATE]).astype(BF16)
            for start in range(0, cols, chunk):
                here = slice(start, start + chunk)
                grown = dot(column.astype(BF16), pe[0, :, here])
                pacc[rows, here] += grown * dot(cross, pv[0, :, here])

    for n in range(7, 12):
        loads[n].wait()
    limits, owners, edge = [], [], jnp.int32(0)
    for k in range(slots):
        which = pack_ref[0, k]
        there = which >= 0
        which = jnp.maximum(which, 0)
        owners.append(jnp.where(there, prm_ref[which], -1))
        limits.append(edge)
        edge = edge + jnp.where(there, len_ref[which], 0)
    limits.append(edge)

    rbc[0 : 2 * TILE, :] = jnp.zeros((2 * TILE, 2 * STATE), BF16)
    rv[0:2] = jnp.zeros((2, TILE, cb), BF16)
    rtot[0:2] = jnp.zeros((2, 8, cb), F32)
    parts = split(rdec_ref[...], 3)
    rdecs[:, 0 : 2 * TILE] = jnp.zeros((4 * head_rows, 2 * TILE), BF16)
    rdecs[:, 2 * TILE :] = jnp.concatenate(parts + [jnp.zeros_like(parts[0])], axis=0).astype(BF16)
    my_cols = pl.ds(pl.multiple_of(me * cb, cb), cb)
    loads[2].wait()
    loads[3].wait()

    def prepare(tile):
        base = pl.multiple_of(tile * TILE, TILE)
        rows = pl.ds(base, TILE)
        place = base + iota((8, TILE), 1)
        start = jnp.zeros((8, TILE), jnp.int32)
        owner = jnp.full((8, TILE), -1, jnp.int32)
        for k in range(slots):
            start = jnp.where(place >= limits[k], limits[k], start)
            owner = jnp.where((place >= limits[k]) & (place < limits[k + 1]), owners[k], owner)
        start = jnp.where(place >= limits[slots], limits[slots], start) - base

        j = iota((3 * TILE, TILE), 0) - 2 * TILE
        i = iota((3 * TILE, TILE), 1)
        ordered = j <= i
        in_slot = jnp.where(ordered & (j >= start[0:1]), 1.0, 0.0)
        in_tile = jnp.where(ordered & (j >= 0), 1.0, 0.0)
        sums = dot(rdecs[:, pl.ds(base, 3 * TILE)], jnp.concatenate([in_slot, in_tile], axis=1).astype(BF16))
        sums = sums[:head_rows] + sums[head_rows : 2 * head_rows] + sums[2 * head_rows : 3 * head_rows]
        gain, c2 = sums[:, :TILE] * LOG2E, sums[:, TILE:] * LOG2E
        dt = rdt[:, rows]
        where_rows = jnp.where(iota((8, TILE), 0) == 0, start, owner).astype(F32)
        stack = [c2] + split(jnp.exp2(c2), 2) + split(jnp.exp2(c2[:, TILE - 1 :] - c2) * dt, 2)
        stack += split(jnp.exp2(gain), 2) + [where_rows]
        stack += [jnp.zeros((TILE - 7 * head_rows - 8, TILE), F32)]
        column = jnp.concatenate(stack, axis=0).T
        wide = dot(column.astype(BF16), re[1])
        last = dot(column[TILE - 8 :].astype(BF16), re[0])
        scaled = (rx[rows, :].astype(F32) * wide).astype(BF16)
        return column, jnp.log2(dt) - c2, scaled, jnp.broadcast_to(last[7:8], (8, cb))

    def prepare_some(step, carry):
        places = [step * together + n for n in range(together)]
        made = [prepare(tile) for tile in places]
        for tile, (column, row_form, scaled, last) in zip(places, made):
            rt[tile] = column
            rrow[tile] = row_form
            rv[tile + 2] = scaled
            rtot[tile + 2] = last
        return carry

    def within(tile):
        base = pl.multiple_of(tile * TILE, TILE)
        rows = pl.ds(base, TILE)
        column = rt[tile]
        x_tile = rx[rows, :]
        grown = dot(column.astype(BF16), re[0])
        c_rows = rbc[pl.ds(base + 2 * TILE, TILE), STATE:]
        scores = dot_nt(c_rows, rbc[pl.ds(base, 3 * TILE), :STATE])
        j = iota((TILE, 3 * TILE), 1) - 2 * TILE
        first = column[:, 7 * head_rows : 7 * head_rows + 1].astype(jnp.int32)
        seen = (j <= iota((TILE, 3 * TILE), 0)) & (j >= first)
        bias = jnp.where(seen[:, 2 * TILE :], 0.0, -1e30)
        cross = jnp.where(seen[:, : 2 * TILE], scores[:, : 2 * TILE], 0.0).astype(BF16)
        earlier = dot(cross[:, TILE:], rv[tile + 1]) + rtot[tile + 1, 0:1] * dot(cross[:, :TILE], rv[tile])
        pieces = diagonal(column, rrow[tile], bias, scores[:, 2 * TILE :], x_tile, block_heads)
        skip = dwide[0:1, my_cols]
        return jnp.concatenate(pieces, axis=1) + grown * earlier + skip * x_tile.astype(F32)

    def response_tiles(step, carry):
        places = [step * 2 + n for n in range(2)]
        made = [within(tile) for tile in places]
        for tile, total in zip(places, made):
            racc[pl.ds(pl.multiple_of(tile * TILE, TILE), TILE), :] = total
        return carry

    together = 4
    lax.fori_loop(0, tiles // together, prepare_some, 0)

    share = tiles // 8
    lax.fori_loop(0, share, response_tiles, 0)

    for step in range(1, seqs):
        state_copy(step).wait_recv()
    ahead = jnp.zeros((STATE, cb), F32)
    for s in range(seqs):
        pbuf[s] = ahead.astype(BF16)
        decay = arecv[s, STATE:, :].astype(F32)
        ahead = (decay[0:1] + decay[1:2]) * ahead + arecv[s, 0:STATE, :].astype(F32)
    seeds[g] = ahead.astype(BF16)

    def pass_on(level, distance, up):
        if up:
            @pl.when(z < levels - 1)
            def _():
                seed_copy(level, g + 2, up_send.at[distance]).start()
        else:
            @pl.when(z > 0)
            def _():
                seed_copy(level, g - 2, down_send.at[distance]).start()

    pass_on(z, 0, True)
    pass_on(z, 0, False)
    seed_copy(z, twin, tu_send.at[0]).start()
    for step in range(1, seqs):
        peer, copy = prefix_copy(step)

        @pl.when(peer > 0)
        def _():
            copy.start()

    precv[me] = pbuf[me]

    def relay(distance):
        @pl.when(z >= distance)
        def _():
            seed_copy(z - distance, twin, tu_send.at[distance]).wait_recv()
            pass_on(z - distance, distance, True)
            seed_copy(z - distance, twin, tu_send.at[distance]).start()

        @pl.when(z + distance < levels)
        def _():
            seed_copy(z + distance, twin, td_send.at[distance]).wait_recv()
            pass_on(z + distance, distance, False)
            seed_copy(z + distance, twin, td_send.at[distance]).start()

    lax.fori_loop(share, 2 * share, response_tiles, 0)
    relay(1)
    lax.fori_loop(2 * share, 3 * share, response_tiles, 0)
    if levels > 2:
        relay(2)
    lax.fori_loop(3 * share, 4 * share, response_tiles, 0)

    for step in range(1, seqs):
        copy = prefix_copy(step)[1]

        @pl.when(me > 0)
        def _():
            copy.wait_recv()

    @pl.when(me == 0)
    def _():
        for s in range(seqs):
            precv[s] = jnp.zeros((STATE, cb), BF16)

    p_outs = []
    for t in range(2):
        rows = slice(t * TILE, (t + 1) * TILE)
        narrow = pt[2 * t].astype(BF16)
        for s in range(seqs):
            here = slice(s * cb, (s + 1) * cb)
            grown = dot(narrow, pe[0, :, here])
            if t == 1:
                grown = grown * ptot[0, 0:1, here]
            carried = grown * dot(pbc[rows, STATE:], precv[s])
            pout[rows, here] = (pacc[rows, here] + carried).astype(BF16)
        p_outs.append(pltpu.make_async_copy(pout.at[rows], pout_hbm.at[rows], out_sem.at[tiles + t]))
        p_outs[-1].start()

    for distance in range(3, levels):
        relay(distance)
    for level in range(levels):
        which = level * 2 + 1 - core
        pltpu.make_async_remote_copy(
            src_ref=seeds.at[which], dst_ref=seeds.at[which], send_sem=tu_send.at[0], recv_sem=g_recv.at[which],
            device_id={"grp": twin}, device_id_type=MESH).wait_recv()

    def out_copy(tile):
        rows = pl.ds(pl.multiple_of(tile * TILE, TILE), TILE)
        return pltpu.make_async_copy(rout.at[rows], rout_hbm.at[rows], out_sem.at[tile])

    def seeded(tile):
        base = pl.multiple_of(tile * TILE, TILE)
        column = rt[tile]
        owner = column[:, 7 * head_rows + 1 : 7 * head_rows + 2].astype(jnp.int32)
        c_rows = rbc[pl.ds(base + 2 * TILE, TILE), STATE:].astype(F32)
        batch = 8 if grps % 8 == 0 else 2
        total = jnp.zeros((TILE, cb), F32)
        for q in range(0, grps, batch):
            chosen = [jnp.where(owner == q + n, c_rows, 0.0) for n in range(batch)]
            table = seeds[q : q + batch].reshape(batch * STATE, cb)
            total = total + dot(jnp.concatenate(chosen, axis=1).astype(BF16), table)
        result = racc[pl.ds(base, TILE), :] + dot(column.astype(BF16), re[2]) * total
        return jnp.where(owner >= 0, result, 0.0).astype(BF16)

    def seed_tiles(step, carry):
        places = [step * 2 + n for n in range(2)]
        made = [seeded(tile) for tile in places]
        for tile, result in zip(places, made):
            rout[pl.ds(pl.multiple_of(tile * TILE, TILE), TILE), :] = result
            out_copy(tile).start()
        return carry

    lax.fori_loop(0, tiles // 2, seed_tiles, 0)

    for step in range(1, seqs):
        state_copy(step).wait_send()
        peer, copy = prefix_copy(step)

        @pl.when(peer > 0)
        def _():
            copy.wait_send()

    for distance in range(levels):
        @pl.when((z >= distance) & (z < levels - 1))
        def _():
            seed_copy(z - distance, g + 2, up_send.at[distance]).wait_send()

        @pl.when((z + distance < levels) & (z > 0))
        def _():
            seed_copy(z + distance, g - 2, down_send.at[distance]).wait_send()

        @pl.when(z >= distance)
        def _():
            seed_copy(z - distance, twin, tu_send.at[distance]).wait_send()

        if distance > 0:
            @pl.when(z + distance < levels)
            def _():
                seed_copy(z + distance, twin, td_send.at[distance]).wait_send()

    for copy in p_outs:
        copy.wait()

    def out_wait(tile, carry):
        out_copy(tile).wait()
        return carry

    lax.fori_loop(0, tiles, out_wait, 0)


def on_device(
    p_x, p_bc, p_dt, p_decay, r_x, r_bc, r_dt, r_decay, pack_list, resp_len, resp_prompt, d_skip
):
    seqs, grps = lax.axis_size("seq"), lax.axis_size("grp")
    heads = p_dt.shape[1]
    block_heads = heads // seqs
    head_rows = max(8, block_heads)
    slots = pack_list.shape[1]
    tiles = r_x.shape[0] // TILE
    cols, cb = heads * CHANNELS, block_heads * CHANNELS
    if head_rows > block_heads:
        extra = ((0, head_rows - block_heads), (0, 0))
        r_dt, r_decay = jnp.pad(r_dt, extra, constant_values=1.0), jnp.pad(r_decay, extra)
    sizes = (seqs, grps, heads, block_heads, head_rows, slots, tiles)
    levels = grps // 2
    anywhere = pl.BlockSpec(memory_space=pl.ANY)
    dma = pltpu.SemaphoreType.DMA
    p_out, r_out = pl.pallas_call(
        functools.partial(kernel, sizes),
        out_shape=(
            jax.ShapeDtypeStruct((2 * TILE, cols), BF16),
            jax.ShapeDtypeStruct((tiles * TILE, cb), BF16),
        ),
        in_specs=[pl.BlockSpec(memory_space=pltpu.HBM)] * 12,
        out_specs=(anywhere, anywhere),
        scratch_shapes=[
            pltpu.VMEM(p_dt.shape[1:], F32),
            pltpu.VMEM(p_decay.shape[1:], F32),
            pltpu.VMEM(r_dt.shape, F32),
            pltpu.VMEM(r_decay.shape, F32),
            pltpu.SMEM(pack_list.shape, jnp.int32),
            pltpu.SMEM(resp_len.shape, jnp.int32),
            pltpu.SMEM(resp_prompt.shape, jnp.int32),
            pltpu.VMEM((1, heads), F32),
            pltpu.VMEM((tiles, head_rows, TILE), F32),
            pltpu.VMEM((2 * TILE, cols), BF16),
            pltpu.VMEM((2 * TILE, 2 * STATE), BF16),
            pltpu.VMEM((tiles * TILE, cb), BF16),
            pltpu.VMEM(((tiles + 2) * TILE, 2 * STATE), BF16),
            pltpu.VMEM((2, TILE, cols), BF16),
            pltpu.VMEM((4, TILE, TILE), F32),
            pltpu.VMEM((2, TILE, cols), BF16),
            pltpu.VMEM((2, 8, cols), F32),
            pltpu.VMEM((2 * TILE, cols), F32),
            pltpu.VMEM((8, cols), F32),
            pltpu.VMEM((tiles + 2, TILE, cb), BF16),
            pltpu.VMEM((tiles, TILE, TILE), F32),
            pltpu.VMEM((3, TILE, cb), BF16),
            pltpu.VMEM((tiles + 2, 8, cb), F32),
            pltpu.VMEM((tiles * TILE, cb), F32),
            pltpu.VMEM((4 * head_rows, (tiles + 2) * TILE), BF16),
            pltpu.VMEM((seqs, STATE + 16, cb), BF16),
            pltpu.VMEM((seqs, STATE + 16, cb), BF16),
            pltpu.VMEM((seqs, STATE, cb), BF16),
            pltpu.VMEM((seqs, STATE, cb), BF16),
            pltpu.VMEM((grps, STATE, cb), BF16),
            pltpu.VMEM((2 * TILE, cols), BF16),
            pltpu.VMEM((tiles * TILE, cb), BF16),
            dma((12,)),
            dma((tiles + 2,)),
            dma((seqs,)),
            dma((seqs,)),
            dma((seqs,)),
            dma((seqs,)),
            dma((grps,)),
            dma((levels,)),
            dma((levels,)),
            dma((levels,)),
            dma((levels,)),
        ],
        compiler_params=pltpu.CompilerParams(
            collective_id=0, has_side_effects=True, vmem_limit_bytes=48 * 2**20
        ),
        cost_estimate=pl.CostEstimate(flops=4 * 10**9, bytes_accessed=8 * 10**6, transcendentals=4 * 10**6),
        name="scan_and_seeds",
    )(
        p_x[0], p_bc[0], p_dt[0], p_decay[0], r_x, r_bc, r_dt, r_decay,
        pack_list, resp_len, resp_prompt, d_skip[None],
    )
    return p_out[None], r_out


def solution(mesh):
    placed = (
        P("grp", "seq", None),
        P("grp", "seq", None),
        P("grp", None, "seq"),
        P("grp", None, "seq"),
        P("grp", "seq"),
        P("grp", None),
        P("seq", "grp"),
        P("seq", "grp"),
        P("grp", None),
        P(),
        P(),
        P(),
    )
    return jax.shard_map(
        on_device,
        mesh=mesh,
        in_specs=placed,
        out_specs=(P("grp", "seq", None), P("grp", "seq")),
        check_vma=False,
    )
```

```python
import functools

import jax
import jax.numpy as jnp
from jax import lax
from jax.experimental import pallas as pl
from jax.experimental.pallas import tpu as pltpu
from jax.sharding import PartitionSpec as P

TILE = 128
STATE = 128
CHANNELS = 64
LOG2E = 1.4426950408889634
F32 = jnp.float32
BF16 = jnp.bfloat16
MESH = pl.DeviceIdType.MESH


def dot(a, b):
    return jnp.dot(a, b, preferred_element_type=F32)


def dot_nt(a, b):
    return lax.dot_general(a, b, (((1,), (1,)), ((), ())), preferred_element_type=F32)


def dot_tn(a, b):
    return lax.dot_general(a, b, (((0,), (0,)), ((), ())), preferred_element_type=F32)


def split(value, terms):
    parts = []
    for _ in range(terms):
        part = value.astype(BF16).astype(F32)
        parts.append(part)
        value = value - part
    return parts


def iota(shape, dim):
    return lax.broadcasted_iota(jnp.int32, shape, dim)


def spreader(rows, columns, bases):
    row = iota((rows, columns), 0)
    head = iota((rows, columns), 1) >> 6
    hit = row == head + bases[0]
    for base in bases[1:]:
        hit = hit | (row == head + base)
    return jnp.where(hit, 1.0, 0.0).astype(BF16)


def paired(x_pair):
    first = iota(x_pair.shape, 1) < CHANNELS
    wide = x_pair.astype(F32)
    return jnp.concatenate([jnp.where(first, wide, 0.0), jnp.where(first, 0.0, wide)], axis=0).astype(BF16)


def diagonal(column, row, bias, scores, x_tile, heads):
    pieces = []
    for pair in range(heads // 2):
        mixes = []
        for h in (2 * pair, 2 * pair + 1):
            power = column[:, h : h + 1] + (row[h : h + 1, :] + bias)
            mixes.append((jnp.exp2(power) * scores).astype(BF16))
        x_pair = x_tile[:, pair * 2 * CHANNELS : (pair + 1) * 2 * CHANNELS]
        pieces.append(dot(jnp.concatenate(mixes, axis=1), paired(x_pair)))
    return pieces


def kernel(
    sizes,
    px_hbm, pbc_hbm, pdt_hbm, pdec_hbm, rx_hbm, rbc_hbm, rdt_hbm, rdec_hbm, pack_hbm, len_hbm, prm_hbm, d_hbm,
    pout_hbm, rout_hbm,
    pdt_ref, pdec_ref, rdt, rdec_ref, pack_ref, len_ref, prm_ref, d_ref, rrow,
    px, pbc, rx, rbc, pv, pt, pe, ptot, pacc, dwide, rv, rt, re, rtot, racc, rdecs,
    abuf, arecv, pbuf, precv, seeds, pout, rout,
    in_sem, out_sem, a_send, a_recv, x_send, x_recv, g_recv, up_send, down_send, tu_send, td_send,
):
    seqs, grps, heads, block_heads, head_rows, slots, tiles = sizes
    cols = heads * CHANNELS
    cb = block_heads * CHANNELS
    me = lax.axis_index("seq")
    g = lax.axis_index("grp")
    z, core = g // 2, lax.rem(g, 2)
    levels = grps // 2
    twin = z * 2 + 1 - core

    loads = [
        pltpu.make_async_copy(px_hbm, px, in_sem.at[0]),
        pltpu.make_async_copy(pbc_hbm, pbc, in_sem.at[1]),
        pltpu.make_async_copy(rx_hbm, rx, in_sem.at[2]),
        pltpu.make_async_copy(rbc_hbm, rbc.at[pl.ds(2 * TILE, tiles * TILE)], in_sem.at[3]),
    ]
    small = [(pdec_hbm, pdec_ref), (pdt_hbm, pdt_ref), (d_hbm, d_ref), (pack_hbm, pack_ref), (len_hbm, len_ref),
             (prm_hbm, prm_ref), (rdec_hbm, rdec_ref), (rdt_hbm, rdt)]
    loads += [pltpu.make_async_copy(src, dst, in_sem.at[4 + n]) for n, (src, dst) in enumerate(small)]
    for n in (4, 5, 0, 1, 6, 7, 8, 9, 10, 11, 2, 3):
        loads[n].start()

    barrier = pltpu.get_barrier_semaphore()
    for step in range(1, seqs):
        pl.semaphore_signal(barrier, inc=1, device_id={"seq": lax.rem(me + step, seqs)}, device_id_type=MESH)
    pl.semaphore_signal(barrier, inc=1, device_id={"grp": twin}, device_id_type=MESH)

    @pl.when(z > 0)
    def _():
        pl.semaphore_signal(barrier, inc=1, device_id={"grp": g - 2}, device_id_type=MESH)

    @pl.when(z < levels - 1)
    def _():
        pl.semaphore_signal(barrier, inc=1, device_id={"grp": g + 2}, device_id_type=MESH)

    pe[0] = spreader(TILE, cols, (32, 64))
    pe[1] = spreader(TILE, cols, (0, 32))
    re[0] = spreader(TILE, cb, (head_rows, 2 * head_rows))
    re[1] = spreader(TILE, cb, (3 * head_rows, 4 * head_rows))
    re[2] = spreader(TILE, cb, (5 * head_rows, 6 * head_rows))
    for n in (4, 5, 6):
        loads[n].wait()
    row8 = iota((8, heads), 0)
    skips = split(jnp.broadcast_to(d_ref[...], (8, heads)), 3)
    skip_rows = jnp.where(row8 == 0, skips[0], jnp.where(row8 == 1, skips[1], jnp.where(row8 == 2, skips[2], 0.0)))
    skip_wide = dot(skip_rows.astype(BF16), spreader(heads, cols, (0,)))
    dwide[...] = jnp.broadcast_to(jnp.sum(skip_wide, axis=0, keepdims=True), (8, cols))

    before = iota((TILE, TILE), 0) <= iota((TILE, TILE), 1)
    upper = jnp.where(before, 1.0, 0.0).astype(BF16)
    low_bias = jnp.where(iota((TILE, TILE), 1) <= iota((TILE, TILE), 0), 0.0, -1e30)

    prow = []
    for t in range(2):
        lanes = slice(t * TILE, (t + 1) * TILE)
        parts = split(pdec_ref[:, lanes], 3)
        sums = dot(jnp.concatenate(parts, axis=0).astype(BF16), upper)
        cum = sums[:heads] + sums[heads : 2 * heads] + sums[2 * heads :]
        dt = pdt_ref[:, lanes]
        c2 = cum * LOG2E
        prow.append(jnp.log2(dt) - c2)
        grown = split(jnp.exp2(c2), 2)
        weight = split(jnp.exp2(c2[:, TILE - 1 :] - c2) * dt, 2)
        fill = jnp.zeros((TILE - 3 * heads, TILE), F32)
        pt[2 * t] = jnp.concatenate([c2] + grown + [fill], axis=0).T
        fill = jnp.zeros((TILE - 2 * heads, TILE), F32)
        pt[2 * t + 1] = jnp.concatenate(weight + [fill], axis=0).T
    loads[0].wait()
    loads[1].wait()
    chunk = min(cols, 512)
    for t in range(2):
        rows = slice(t * TILE, (t + 1) * TILE)
        for start in range(0, cols, chunk):
            here = slice(start, start + chunk)
            wide = dot(pt[2 * t + 1].astype(BF16), pe[1, :, here])
            pv[t, :, here] = (px[rows, here].astype(F32) * wide).astype(BF16)
            last = dot(pt[2 * t, TILE - 8 :, :].astype(BF16), pe[0, :, here])
            ptot[t, :, here] = jnp.broadcast_to(last[7:8], (8, chunk))
    for s in range(seqs):
        here = slice(s * cb, (s + 1) * cb)
        t0, t1 = ptot[0, 0:1, here], ptot[1, 0:1, here]
        ended = t1 * dot_tn(pbc[0:TILE, :STATE], pv[0, :, here]) + dot_tn(pbc[TILE:, :STATE], pv[1, :, here])
        abuf[s, 0:STATE, :] = ended.astype(BF16)
        hi, lo = split(t0 * t1, 2)
        row = iota((16, cb), 0)
        abuf[s, STATE:, :] = jnp.where(row == 0, hi, jnp.where(row == 1, lo, 0.0)).astype(BF16)

    pl.semaphore_wait(barrier, seqs + jnp.where(z > 0, 1, 0) + jnp.where(z < levels - 1, 1, 0))

    def state_copy(step):
        peer = lax.rem(me + step, seqs)
        return pltpu.make_async_remote_copy(
            src_ref=abuf.at[peer], dst_ref=arecv.at[me], send_sem=a_send.at[step], recv_sem=a_recv.at[step],
            device_id={"seq": peer}, device_id_type=MESH)

    def prefix_copy(step):
        peer = lax.rem(me + step, seqs)
        return peer, pltpu.make_async_remote_copy(
            src_ref=pbuf.at[peer], dst_ref=precv.at[me], send_sem=x_send.at[step], recv_sem=x_recv.at[step],
            device_id={"seq": peer}, device_id_type=MESH)

    def seed_copy(level, target, send_sem):
        which = level * 2 + core
        return pltpu.make_async_remote_copy(
            src_ref=seeds.at[which], dst_ref=seeds.at[which], send_sem=send_sem, recv_sem=g_recv.at[which],
            device_id={"grp": target}, device_id_type=MESH)

    for step in range(1, seqs):
        state_copy(step).start()
    arecv[me] = abuf[me]

    for t in range(2):
        rows = slice(t * TILE, (t + 1) * TILE)
        b_rows, c_rows = pbc[rows, :STATE], pbc[rows, STATE:]
        scores = dot_nt(c_rows, b_rows)
        column = pt[2 * t]
        x_tile = px[rows, :]
        pieces = diagonal(column, prow[t], low_bias, scores, x_tile, heads)
        for pair, piece in enumerate(pieces):
            here = slice(pair * 2 * CHANNELS, (pair + 1) * 2 * CHANNELS)
            pacc[rows, here] = piece + dwide[0:1, here] * x_tile[:, here].astype(F32)
        if t == 1:
            cross = dot_nt(c_rows, pbc[0:TILE, :STATE]).astype(BF16)
            for start in range(0, cols, chunk):
                here = slice(start, start + chunk)
                grown = dot(column.astype(BF16), pe[0, :, here])
                pacc[rows, here] += grown * dot(cross, pv[0, :, here])

    for step in range(1, seqs):
        state_copy(step).wait_recv()
    ahead = jnp.zeros((STATE, cb), F32)
    for s in range(seqs):
        pbuf[s] = ahead.astype(BF16)
        decay = arecv[s, STATE:, :].astype(F32)
        ahead = (decay[0:1] + decay[1:2]) * ahead + arecv[s, 0:STATE, :].astype(F32)
    seeds[g] = ahead.astype(BF16)

    def pass_on(level, distance, up):
        if up:
            @pl.when(z < levels - 1)
            def _():
                seed_copy(level, g + 2, up_send.at[distance]).start()
        else:
            @pl.when(z > 0)
            def _():
                seed_copy(level, g - 2, down_send.at[distance]).start()

    pass_on(z, 0, True)
    pass_on(z, 0, False)
    seed_copy(z, twin, tu_send.at[0]).start()
    for step in range(1, seqs):
        peer, copy = prefix_copy(step)

        @pl.when(peer > 0)
        def _():
            copy.start()

    precv[me] = pbuf[me]

    for n in range(7, 12):
        loads[n].wait()
    limits, owners, edge = [], [], jnp.int32(0)
    for k in range(slots):
        which = pack_ref[0, k]
        there = which >= 0
        which = jnp.maximum(which, 0)
        owners.append(jnp.where(there, prm_ref[which], -1))
        limits.append(edge)
        edge = edge + jnp.where(there, len_ref[which], 0)
    limits.append(edge)

    rbc[0 : 2 * TILE, :] = jnp.zeros((2 * TILE, 2 * STATE), BF16)
    rv[0:2] = jnp.zeros((2, TILE, cb), BF16)
    rtot[0:2] = jnp.zeros((2, 8, cb), F32)
    parts = split(rdec_ref[...], 3)
    rdecs[:, 0 : 2 * TILE] = jnp.zeros((4 * head_rows, 2 * TILE), BF16)
    rdecs[:, 2 * TILE :] = jnp.concatenate(parts + [jnp.zeros_like(parts[0])], axis=0).astype(BF16)
    my_cols = pl.ds(pl.multiple_of(me * cb, cb), cb)
    loads[2].wait()
    loads[3].wait()

    def prepare(tile):
        base = pl.multiple_of(tile * TILE, TILE)
        rows = pl.ds(base, TILE)
        place = base + iota((8, TILE), 1)
        start = jnp.zeros((8, TILE), jnp.int32)
        owner = jnp.full((8, TILE), -1, jnp.int32)
        for k in range(slots):
            start = jnp.where(place >= limits[k], limits[k], start)
            owner = jnp.where((place >= limits[k]) & (place < limits[k + 1]), owners[k], owner)
        start = jnp.where(place >= limits[slots], limits[slots], start) - base

        j = iota((3 * TILE, TILE), 0) - 2 * TILE
        i = iota((3 * TILE, TILE), 1)
        ordered = j <= i
        in_slot = jnp.where(ordered & (j >= start[0:1]), 1.0, 0.0)
        in_tile = jnp.where(ordered & (j >= 0), 1.0, 0.0)
        sums = dot(rdecs[:, pl.ds(base, 3 * TILE)], jnp.concatenate([in_slot, in_tile], axis=1).astype(BF16))
        sums = sums[:head_rows] + sums[head_rows : 2 * head_rows] + sums[2 * head_rows : 3 * head_rows]
        gain, c2 = sums[:, :TILE] * LOG2E, sums[:, TILE:] * LOG2E
        dt = rdt[:, rows]
        where_rows = jnp.where(iota((8, TILE), 0) == 0, start, owner).astype(F32)
        stack = [c2] + split(jnp.exp2(c2), 2) + split(jnp.exp2(c2[:, TILE - 1 :] - c2) * dt, 2)
        stack += split(jnp.exp2(gain), 2) + [where_rows]
        stack += [jnp.zeros((TILE - 7 * head_rows - 8, TILE), F32)]
        column = jnp.concatenate(stack, axis=0).T
        wide = dot(column.astype(BF16), re[1])
        last = dot(column[TILE - 8 :].astype(BF16), re[0])
        scaled = (rx[rows, :].astype(F32) * wide).astype(BF16)
        return column, jnp.log2(dt) - c2, scaled, jnp.broadcast_to(last[7:8], (8, cb))

    def prepare_some(step, carry):
        places = [step * together + n for n in range(together)]
        made = [prepare(tile) for tile in places]
        for tile, (column, row_form, scaled, last) in zip(places, made):
            rt[tile] = column
            rrow[tile] = row_form
            rv[tile + 2] = scaled
            rtot[tile + 2] = last
        return carry

    def within(tile):
        base = pl.multiple_of(tile * TILE, TILE)
        rows = pl.ds(base, TILE)
        column = rt[tile]
        x_tile = rx[rows, :]
        grown = dot(column.astype(BF16), re[0])
        c_rows = rbc[pl.ds(base + 2 * TILE, TILE), STATE:]
        scores = dot_nt(c_rows, rbc[pl.ds(base, 3 * TILE), :STATE])
        j = iota((TILE, 3 * TILE), 1) - 2 * TILE
        first = column[:, 7 * head_rows : 7 * head_rows + 1].astype(jnp.int32)
        seen = (j <= iota((TILE, 3 * TILE), 0)) & (j >= first)
        bias = jnp.where(seen[:, 2 * TILE :], 0.0, -1e30)
        cross = jnp.where(seen[:, : 2 * TILE], scores[:, : 2 * TILE], 0.0).astype(BF16)
        earlier = dot(cross[:, TILE:], rv[tile + 1]) + rtot[tile + 1, 0:1] * dot(cross[:, :TILE], rv[tile])
        pieces = diagonal(column, rrow[tile], bias, scores[:, 2 * TILE :], x_tile, block_heads)
        skip = dwide[0:1, my_cols]
        return jnp.concatenate(pieces, axis=1) + grown * earlier + skip * x_tile.astype(F32)

    def response_tiles(step, carry):
        places = [step * 2 + n for n in range(2)]
        made = [within(tile) for tile in places]
        for tile, total in zip(places, made):
            racc[pl.ds(pl.multiple_of(tile * TILE, TILE), TILE), :] = total
        return carry

    def relay(distance):
        @pl.when(z >= distance)
        def _():
            seed_copy(z - distance, twin, tu_send.at[distance]).wait_recv()
            pass_on(z - distance, distance, True)
            seed_copy(z - distance, twin, tu_send.at[distance]).start()

        @pl.when(z + distance < levels)
        def _():
            seed_copy(z + distance, twin, td_send.at[distance]).wait_recv()
            pass_on(z + distance, distance, False)
            seed_copy(z + distance, twin, td_send.at[distance]).start()

    together = 4
    share = tiles // 8
    lax.fori_loop(0, tiles // together, prepare_some, 0)
    relay(1)
    lax.fori_loop(0, share, response_tiles, 0)
    for distance in range(2, levels):
        relay(distance)
        if distance < 4:
            lax.fori_loop((distance - 1) * share, distance * share, response_tiles, 0)
    lax.fori_loop((min(levels, 4) - 1) * share, 4 * share, response_tiles, 0)

    for step in range(1, seqs):
        copy = prefix_copy(step)[1]

        @pl.when(me > 0)
        def _():
            copy.wait_recv()

    @pl.when(me == 0)
    def _():
        for s in range(seqs):
            precv[s] = jnp.zeros((STATE, cb), BF16)

    p_outs = []
    for t in range(2):
        rows = slice(t * TILE, (t + 1) * TILE)
        narrow = pt[2 * t].astype(BF16)
        for s in range(seqs):
            here = slice(s * cb, (s + 1) * cb)
            grown = dot(narrow, pe[0, :, here])
            if t == 1:
                grown = grown * ptot[0, 0:1, here]
            carried = grown * dot(pbc[rows, STATE:], precv[s])
            pout[rows, here] = (pacc[rows, here] + carried).astype(BF16)
        p_outs.append(pltpu.make_async_copy(pout.at[rows], pout_hbm.at[rows], out_sem.at[tiles + t]))
        p_outs[-1].start()

    for level in range(levels):
        which = level * 2 + 1 - core
        pltpu.make_async_remote_copy(
            src_ref=seeds.at[which], dst_ref=seeds.at[which], send_sem=tu_send.at[0], recv_sem=g_recv.at[which],
            device_id={"grp": twin}, device_id_type=MESH).wait_recv()

    def out_copy(tile):
        rows = pl.ds(pl.multiple_of(tile * TILE, TILE), TILE)
        return pltpu.make_async_copy(rout.at[rows], rout_hbm.at[rows], out_sem.at[tile])

    def seeded(tile):
        base = pl.multiple_of(tile * TILE, TILE)
        column = rt[tile]
        owner = column[:, 7 * head_rows + 1 : 7 * head_rows + 2].astype(jnp.int32)
        c_rows = rbc[pl.ds(base + 2 * TILE, TILE), STATE:].astype(F32)
        batch = 8 if grps % 8 == 0 else 2
        total = jnp.zeros((TILE, cb), F32)
        for q in range(0, grps, batch):
            chosen = [jnp.where(owner == q + n, c_rows, 0.0) for n in range(batch)]
            table = seeds[q : q + batch].reshape(batch * STATE, cb)
            total = total + dot(jnp.concatenate(chosen, axis=1).astype(BF16), table)
        result = racc[pl.ds(base, TILE), :] + dot(column.astype(BF16), re[2]) * total
        return jnp.where(owner >= 0, result, 0.0).astype(BF16)

    def seed_tiles(step, carry):
        places = [step * 2 + n for n in range(2)]
        made = [seeded(tile) for tile in places]
        for tile, result in zip(places, made):
            rout[pl.ds(pl.multiple_of(tile * TILE, TILE), TILE), :] = result
            out_copy(tile).start()
        return carry

    lax.fori_loop(0, tiles // 2, seed_tiles, 0)

    for step in range(1, seqs):
        state_copy(step).wait_send()
        peer, copy = prefix_copy(step)

        @pl.when(peer > 0)
        def _():
            copy.wait_send()

    for distance in range(levels):
        @pl.when((z >= distance) & (z < levels - 1))
        def _():
            seed_copy(z - distance, g + 2, up_send.at[distance]).wait_send()

        @pl.when((z + distance < levels) & (z > 0))
        def _():
            seed_copy(z + distance, g - 2, down_send.at[distance]).wait_send()

        @pl.when(z >= distance)
        def _():
            seed_copy(z - distance, twin, tu_send.at[distance]).wait_send()

        if distance > 0:
            @pl.when(z + distance < levels)
            def _():
                seed_copy(z + distance, twin, td_send.at[distance]).wait_send()

    for copy in p_outs:
        copy.wait()

    def out_wait(tile, carry):
        out_copy(tile).wait()
        return carry

    lax.fori_loop(0, tiles, out_wait, 0)


def on_device(
    p_x, p_bc, p_dt, p_decay, r_x, r_bc, r_dt, r_decay, pack_list, resp_len, resp_prompt, d_skip
):
    seqs, grps = lax.axis_size("seq"), lax.axis_size("grp")
    heads = p_dt.shape[1]
    block_heads = heads // seqs
    head_rows = max(8, block_heads)
    slots = pack_list.shape[1]
    tiles = r_x.shape[0] // TILE
    cols, cb = heads * CHANNELS, block_heads * CHANNELS
    if head_rows > block_heads:
        extra = ((0, head_rows - block_heads), (0, 0))
        r_dt, r_decay = jnp.pad(r_dt, extra, constant_values=1.0), jnp.pad(r_decay, extra)
    sizes = (seqs, grps, heads, block_heads, head_rows, slots, tiles)
    levels = grps // 2
    anywhere = pl.BlockSpec(memory_space=pl.ANY)
    dma = pltpu.SemaphoreType.DMA
    p_out, r_out = pl.pallas_call(
        functools.partial(kernel, sizes),
        out_shape=(
            jax.ShapeDtypeStruct((2 * TILE, cols), BF16),
            jax.ShapeDtypeStruct((tiles * TILE, cb), BF16),
        ),
        in_specs=[pl.BlockSpec(memory_space=pltpu.HBM)] * 12,
        out_specs=(anywhere, anywhere),
        scratch_shapes=[
            pltpu.VMEM(p_dt.shape[1:], F32),
            pltpu.VMEM(p_decay.shape[1:], F32),
            pltpu.VMEM(r_dt.shape, F32),
            pltpu.VMEM(r_decay.shape, F32),
            pltpu.SMEM(pack_list.shape, jnp.int32),
            pltpu.SMEM(resp_len.shape, jnp.int32),
            pltpu.SMEM(resp_prompt.shape, jnp.int32),
            pltpu.VMEM((1, heads), F32),
            pltpu.VMEM((tiles, head_rows, TILE), F32),
            pltpu.VMEM((2 * TILE, cols), BF16),
            pltpu.VMEM((2 * TILE, 2 * STATE), BF16),
            pltpu.VMEM((tiles * TILE, cb), BF16),
            pltpu.VMEM(((tiles + 2) * TILE, 2 * STATE), BF16),
            pltpu.VMEM((2, TILE, cols), BF16),
            pltpu.VMEM((4, TILE, TILE), F32),
            pltpu.VMEM((2, TILE, cols), BF16),
            pltpu.VMEM((2, 8, cols), F32),
            pltpu.VMEM((2 * TILE, cols), F32),
            pltpu.VMEM((8, cols), F32),
            pltpu.VMEM((tiles + 2, TILE, cb), BF16),
            pltpu.VMEM((tiles, TILE, TILE), F32),
            pltpu.VMEM((3, TILE, cb), BF16),
            pltpu.VMEM((tiles + 2, 8, cb), F32),
            pltpu.VMEM((tiles * TILE, cb), F32),
            pltpu.VMEM((4 * head_rows, (tiles + 2) * TILE), BF16),
            pltpu.VMEM((seqs, STATE + 16, cb), BF16),
            pltpu.VMEM((seqs, STATE + 16, cb), BF16),
            pltpu.VMEM((seqs, STATE, cb), BF16),
            pltpu.VMEM((seqs, STATE, cb), BF16),
            pltpu.VMEM((grps, STATE, cb), BF16),
            pltpu.VMEM((2 * TILE, cols), BF16),
            pltpu.VMEM((tiles * TILE, cb), BF16),
            dma((12,)),
            dma((tiles + 2,)),
            dma((seqs,)),
            dma((seqs,)),
            dma((seqs,)),
            dma((seqs,)),
            dma((grps,)),
            dma((levels,)),
            dma((levels,)),
            dma((levels,)),
            dma((levels,)),
        ],
        compiler_params=pltpu.CompilerParams(
            collective_id=0, has_side_effects=True, vmem_limit_bytes=63 * 2**20
        ),
        cost_estimate=pl.CostEstimate(flops=4 * 10**9, bytes_accessed=8 * 10**6, transcendentals=4 * 10**6),
        name="scan_and_seeds",
    )(
        p_x[0], p_bc[0], p_dt[0], p_decay[0], r_x, r_bc, r_dt, r_decay,
        pack_list, resp_len, resp_prompt, d_skip[None],
    )
    return p_out[None], r_out


def solution(mesh):
    placed = (
        P("grp", "seq", None),
        P("grp", "seq", None),
        P("grp", None, "seq"),
        P("grp", None, "seq"),
        P("grp", "seq"),
        P("grp", None),
        P("seq", "grp"),
        P("seq", "grp"),
        P("grp", None),
        P(),
        P(),
        P(),
    )
    return jax.shard_map(
        on_device,
        mesh=mesh,
        in_specs=placed,
        out_specs=(P("grp", "seq", None), P("grp", "seq")),
        check_vma=False,
    )
```

```python
import functools

import jax
import jax.numpy as jnp
from jax import lax
from jax.experimental import pallas as pl
from jax.experimental.pallas import tpu as pltpu
from jax.sharding import PartitionSpec as P

TILE = 128
STATE = 128
CHANNELS = 64
LOG2E = 1.4426950408889634
F32 = jnp.float32
BF16 = jnp.bfloat16
MESH = pl.DeviceIdType.MESH


def dot(a, b):
    return jnp.dot(a, b, preferred_element_type=F32)


def dot_nt(a, b):
    return lax.dot_general(a, b, (((1,), (1,)), ((), ())), preferred_element_type=F32)


def dot_tn(a, b):
    return lax.dot_general(a, b, (((0,), (0,)), ((), ())), preferred_element_type=F32)


def split(value, terms):
    parts = []
    for _ in range(terms):
        part = value.astype(BF16).astype(F32)
        parts.append(part)
        value = value - part
    return parts


def iota(shape, dim):
    return lax.broadcasted_iota(jnp.int32, shape, dim)


def spreader(rows, columns, bases):
    row = iota((rows, columns), 0)
    head = iota((rows, columns), 1) >> 6
    hit = row == head + bases[0]
    for base in bases[1:]:
        hit = hit | (row == head + base)
    return jnp.where(hit, 1.0, 0.0).astype(BF16)


def paired(x_pair):
    first = jnp.where(iota(x_pair.shape, 1) < CHANNELS, 1.0, 0.0).astype(BF16)
    second = jnp.where(iota(x_pair.shape, 1) < CHANNELS, 0.0, 1.0).astype(BF16)
    return jnp.concatenate([x_pair * first, x_pair * second], axis=0)


def diagonal(column, row, bias, scores, x_tile, heads):
    pieces = []
    for pair in range(heads // 2):
        mixes = []
        for h in (2 * pair, 2 * pair + 1):
            power = column[:, h : h + 1] + (row[h : h + 1, :] + bias)
            mixes.append((jnp.exp2(power) * scores).astype(BF16))
        x_pair = x_tile[:, pair * 2 * CHANNELS : (pair + 1) * 2 * CHANNELS]
        pieces.append(dot(jnp.concatenate(mixes, axis=1), paired(x_pair)))
    return pieces


def kernel(
    sizes,
    px_hbm, pbc_hbm, pdt_hbm, pdec_hbm, rx_hbm, rbc_hbm, rdt_hbm, rdec_hbm, pack_hbm, len_hbm, prm_hbm, d_hbm,
    pout_hbm, rout_hbm,
    pdt_ref, pdec_ref, rdt, rdec_ref, pack_ref, len_ref, prm_ref, d_ref, rrow,
    px, pbc, rx, rbc, pv, pt, pe, ptot, pacc, dwide, rv, rt, re, rtot, racc, rdecs,
    abuf, arecv, pbuf, precv, seeds, pout, rout,
    in_sem, out_sem, a_send, a_recv, x_send, x_recv, g_recv, up_send, down_send, tu_send, td_send,
):
    seqs, grps, heads, block_heads, head_rows, slots, tiles = sizes
    cols = heads * CHANNELS
    cb = block_heads * CHANNELS
    me = lax.axis_index("seq")
    g = lax.axis_index("grp")
    z, core = g // 2, lax.rem(g, 2)
    levels = grps // 2
    twin = z * 2 + 1 - core

    loads = [
        pltpu.make_async_copy(px_hbm, px, in_sem.at[0]),
        pltpu.make_async_copy(pbc_hbm, pbc, in_sem.at[1]),
        pltpu.make_async_copy(rx_hbm, rx, in_sem.at[2]),
        pltpu.make_async_copy(rbc_hbm, rbc.at[pl.ds(2 * TILE, tiles * TILE)], in_sem.at[3]),
    ]
    small = [(pdec_hbm, pdec_ref), (pdt_hbm, pdt_ref), (d_hbm, d_ref), (pack_hbm, pack_ref), (len_hbm, len_ref),
             (prm_hbm, prm_ref), (rdec_hbm, rdec_ref), (rdt_hbm, rdt)]
    loads += [pltpu.make_async_copy(src, dst, in_sem.at[4 + n]) for n, (src, dst) in enumerate(small)]
    for n in (4, 5, 0, 1, 6, 7, 8, 9, 10, 11, 2, 3):
        loads[n].start()

    barrier = pltpu.get_barrier_semaphore()
    for step in range(1, seqs):
        pl.semaphore_signal(barrier, inc=1, device_id={"seq": lax.rem(me + step, seqs)}, device_id_type=MESH)
    pl.semaphore_signal(barrier, inc=1, device_id={"grp": twin}, device_id_type=MESH)

    @pl.when(z > 0)
    def _():
        pl.semaphore_signal(barrier, inc=1, device_id={"grp": g - 2}, device_id_type=MESH)

    @pl.when(z < levels - 1)
    def _():
        pl.semaphore_signal(barrier, inc=1, device_id={"grp": g + 2}, device_id_type=MESH)

    each = spreader(heads, cols, (0,))
    none = jnp.zeros((heads, cols), BF16)
    pe[0] = jnp.concatenate([none, each, each, none], axis=0)
    pe[1] = jnp.concatenate([each, each, none, none], axis=0)
    re[0] = spreader(TILE, cb, (head_rows, 2 * head_rows))
    re[1] = spreader(TILE, cb, (3 * head_rows, 4 * head_rows))
    re[2] = spreader(TILE, cb, (5 * head_rows, 6 * head_rows))
    for n in (4, 5, 6):
        loads[n].wait()
    row8 = iota((8, heads), 0)
    skips = split(jnp.broadcast_to(d_ref[...], (8, heads)), 3)
    skip_rows = jnp.where(row8 == 0, skips[0], jnp.where(row8 == 1, skips[1], jnp.where(row8 == 2, skips[2], 0.0)))
    skip_wide = dot(skip_rows.astype(BF16), each)
    dwide[...] = jnp.broadcast_to(jnp.sum(skip_wide, axis=0, keepdims=True), (8, cols))

    before = iota((TILE, TILE), 0) <= iota((TILE, TILE), 1)
    upper = jnp.where(before, 1.0, 0.0).astype(BF16)
    low_bias = jnp.where(iota((TILE, TILE), 1) <= iota((TILE, TILE), 0), 0.0, -1e30)

    prow = []
    for t in range(2):
        lanes = slice(t * TILE, (t + 1) * TILE)
        parts = split(pdec_ref[:, lanes], 3)
        sums = dot(jnp.concatenate(parts, axis=0).astype(BF16), upper)
        cum = sums[:heads] + sums[heads : 2 * heads] + sums[2 * heads :]
        dt = pdt_ref[:, lanes]
        c2 = cum * LOG2E
        prow.append(jnp.log2(dt) - c2)
        grown = split(jnp.exp2(c2), 2)
        weight = split(jnp.exp2(c2[:, TILE - 1 :] - c2) * dt, 2)
        fill = jnp.zeros((TILE - 3 * heads, TILE), F32)
        pt[2 * t] = jnp.concatenate([c2] + grown + [fill], axis=0).T
        fill = jnp.zeros((TILE - 2 * heads, TILE), F32)
        pt[2 * t + 1] = jnp.concatenate(weight + [fill], axis=0).T
    loads[0].wait()
    loads[1].wait()
    chunk = min(cols, 512)
    for t in range(2):
        rows = slice(t * TILE, (t + 1) * TILE)
        for start in range(0, cols, chunk):
            here = slice(start, start + chunk)
            wide = dot(pt[2 * t + 1].astype(BF16), pe[1, :, here])
            pv[t, :, here] = (px[rows, here].astype(F32) * wide).astype(BF16)
            last = dot(pt[2 * t, TILE - 8 :, :].astype(BF16), pe[0, :, here])
            ptot[t, :, here] = jnp.broadcast_to(last[7:8], (8, chunk))
    for s in range(seqs):
        here = slice(s * cb, (s + 1) * cb)
        t0, t1 = ptot[0, 0:1, here], ptot[1, 0:1, here]
        ended = t1 * dot_tn(pbc[0:TILE, :STATE], pv[0, :, here]) + dot_tn(pbc[TILE:, :STATE], pv[1, :, here])
        abuf[s, 0:STATE, :] = ended.astype(BF16)
        hi, lo = split(t0 * t1, 2)
        row = iota((16, cb), 0)
        abuf[s, STATE:, :] = jnp.where(row == 0, hi, jnp.where(row == 1, lo, 0.0)).astype(BF16)

    pl.semaphore_wait(barrier, seqs + jnp.where(z > 0, 1, 0) + jnp.where(z < levels - 1, 1, 0))

    def state_copy(step):
        peer = lax.rem(me + step, seqs)
        return pltpu.make_async_remote_copy(
            src_ref=abuf.at[peer], dst_ref=arecv.at[me], send_sem=a_send.at[step], recv_sem=a_recv.at[step],
            device_id={"seq": peer}, device_id_type=MESH)

    def prefix_copy(step):
        peer = lax.rem(me + step, seqs)
        return peer, pltpu.make_async_remote_copy(
            src_ref=pbuf.at[peer], dst_ref=precv.at[me], send_sem=x_send.at[step], recv_sem=x_recv.at[step],
            device_id={"seq": peer}, device_id_type=MESH)

    def seed_copy(level, target, send_sem):
        which = level * 2 + core
        return pltpu.make_async_remote_copy(
            src_ref=seeds.at[which], dst_ref=seeds.at[which], send_sem=send_sem, recv_sem=g_recv.at[which],
            device_id={"grp": target}, device_id_type=MESH)

    for step in range(1, seqs):
        state_copy(step).start()
    arecv[me] = abuf[me]

    for t in range(2):
        rows = slice(t * TILE, (t + 1) * TILE)
        b_rows, c_rows = pbc[rows, :STATE], pbc[rows, STATE:]
        scores = dot_nt(c_rows, b_rows)
        column = pt[2 * t]
        x_tile = px[rows, :]
        pieces = diagonal(column, prow[t], low_bias, scores, x_tile, heads)
        for pair, piece in enumerate(pieces):
            here = slice(pair * 2 * CHANNELS, (pair + 1) * 2 * CHANNELS)
            pacc[rows, here] = piece + dwide[0:1, here] * x_tile[:, here].astype(F32)
        if t == 1:
            cross = dot_nt(c_rows, pbc[0:TILE, :STATE]).astype(BF16)
            for start in range(0, cols, chunk):
                here = slice(start, start + chunk)
                grown = dot(column.astype(BF16), pe[0, :, here])
                pacc[rows, here] += grown * dot(cross, pv[0, :, here])

    for step in range(1, seqs):
        state_copy(step).wait_recv()
    ahead = jnp.zeros((STATE, cb), F32)
    for s in range(seqs):
        pbuf[s] = ahead.astype(BF16)
        decay = arecv[s, STATE:, :].astype(F32)
        ahead = (decay[0:1] + decay[1:2]) * ahead + arecv[s, 0:STATE, :].astype(F32)
    seeds[g] = ahead.astype(BF16)

    def pass_on(level, distance, up):
        if up:
            @pl.when(z < levels - 1)
            def _():
                seed_copy(level, g + 2, up_send.at[distance]).start()
        else:
            @pl.when(z > 0)
            def _():
                seed_copy(level, g - 2, down_send.at[distance]).start()

    pass_on(z, 0, True)
    pass_on(z, 0, False)
    seed_copy(z, twin, tu_send.at[0]).start()
    for step in range(1, seqs):
        peer, copy = prefix_copy(step)

        @pl.when(peer > 0)
        def _():
            copy.start()

    precv[me] = pbuf[me]

    for n in range(7, 12):
        loads[n].wait()
    limits, owners, edge = [], [], jnp.int32(0)
    for k in range(slots):
        which = pack_ref[0, k]
        there = which >= 0
        which = jnp.maximum(which, 0)
        owners.append(jnp.where(there, prm_ref[which], -1))
        limits.append(edge)
        edge = edge + jnp.where(there, len_ref[which], 0)
    limits.append(edge)

    rbc[0 : 2 * TILE, :] = jnp.zeros((2 * TILE, 2 * STATE), BF16)
    rv[0:2] = jnp.zeros((2, TILE, cb), BF16)
    rtot[0:2] = jnp.zeros((2, 8, cb), F32)
    parts = split(rdec_ref[...], 3)
    rdecs[:, 0 : 2 * TILE] = jnp.zeros((4 * head_rows, 2 * TILE), BF16)
    rdecs[:, 2 * TILE :] = jnp.concatenate(parts + [jnp.zeros_like(parts[0])], axis=0).astype(BF16)
    my_cols = pl.ds(pl.multiple_of(me * cb, cb), cb)
    loads[2].wait()
    loads[3].wait()

    def prepare(tile):
        base = pl.multiple_of(tile * TILE, TILE)
        rows = pl.ds(base, TILE)
        place = base + iota((8, TILE), 1)
        start = jnp.zeros((8, TILE), jnp.int32)
        owner = jnp.full((8, TILE), -1, jnp.int32)
        for k in range(slots):
            start = jnp.where(place >= limits[k], limits[k], start)
            owner = jnp.where((place >= limits[k]) & (place < limits[k + 1]), owners[k], owner)
        start = jnp.where(place >= limits[slots], limits[slots], start) - base

        j = iota((3 * TILE, TILE), 0) - 2 * TILE
        i = iota((3 * TILE, TILE), 1)
        ordered = j <= i
        in_slot = jnp.where(ordered & (j >= start[0:1]), 1.0, 0.0)
        in_tile = jnp.where(ordered & (j >= 0), 1.0, 0.0)
        sums = dot(rdecs[:, pl.ds(base, 3 * TILE)], jnp.concatenate([in_slot, in_tile], axis=1).astype(BF16))
        sums = sums[:head_rows] + sums[head_rows : 2 * head_rows] + sums[2 * head_rows : 3 * head_rows]
        gain, c2 = sums[:, :TILE] * LOG2E, sums[:, TILE:] * LOG2E
        dt = rdt[:, rows]
        where_rows = jnp.where(iota((8, TILE), 0) == 0, start, owner).astype(F32)
        stack = [c2] + split(jnp.exp2(c2), 2) + split(jnp.exp2(c2[:, TILE - 1 :] - c2) * dt, 2)
        stack += split(jnp.exp2(gain), 2) + [where_rows]
        stack += [jnp.zeros((TILE - 7 * head_rows - 8, TILE), F32)]
        column = jnp.concatenate(stack, axis=0).T
        wide = dot(column.astype(BF16), re[1])
        last = dot(column[TILE - 8 :].astype(BF16), re[0])
        scaled = (rx[rows, :].astype(F32) * wide).astype(BF16)
        return column, jnp.log2(dt) - c2, scaled, jnp.broadcast_to(last[7:8], (8, cb))

    def prepare_some(step, carry):
        places = [step * together + n for n in range(together)]
        made = [prepare(tile) for tile in places]
        for tile, (column, row_form, scaled, last) in zip(places, made):
            rt[tile] = column
            rrow[tile] = row_form
            rv[tile + 2] = scaled
            rtot[tile + 2] = last
        return carry

    def within(tile):
        base = pl.multiple_of(tile * TILE, TILE)
        rows = pl.ds(base, TILE)
        column = rt[tile]
        x_tile = rx[rows, :]
        grown = dot(column.astype(BF16), re[0])
        c_rows = rbc[pl.ds(base + 2 * TILE, TILE), STATE:]
        scores = dot_nt(c_rows, rbc[pl.ds(base, 3 * TILE), :STATE])
        j = iota((TILE, 3 * TILE), 1) - 2 * TILE
        first = column[:, 7 * head_rows : 7 * head_rows + 1].astype(jnp.int32)
        seen = (j <= iota((TILE, 3 * TILE), 0)) & (j >= first)
        bias = jnp.where(seen[:, 2 * TILE :], 0.0, -1e30)
        cross = jnp.where(seen[:, : 2 * TILE], scores[:, : 2 * TILE], 0.0).astype(BF16)
        earlier = dot(cross[:, TILE:], rv[tile + 1]) + rtot[tile + 1, 0:1] * dot(cross[:, :TILE], rv[tile])
        pieces = diagonal(column, rrow[tile], bias, scores[:, 2 * TILE :], x_tile, block_heads)
        skip = dwide[0:1, my_cols]
        return jnp.concatenate(pieces, axis=1) + grown * earlier + skip * x_tile.astype(F32)

    def response_tiles(step, carry):
        places = [step * 2 + n for n in range(2)]
        made = [within(tile) for tile in places]
        for tile, total in zip(places, made):
            racc[pl.ds(pl.multiple_of(tile * TILE, TILE), TILE), :] = total
        return carry

    def relay(distance):
        @pl.when(z >= distance)
        def _():
            seed_copy(z - distance, twin, tu_send.at[distance]).wait_recv()
            pass_on(z - distance, distance, True)
            seed_copy(z - distance, twin, tu_send.at[distance]).start()

        @pl.when(z + distance < levels)
        def _():
            seed_copy(z + distance, twin, td_send.at[distance]).wait_recv()
            pass_on(z + distance, distance, False)
            seed_copy(z + distance, twin, td_send.at[distance]).start()

    together = 4
    share = tiles // 8
    lax.fori_loop(0, tiles // together, prepare_some, 0)
    relay(1)
    lax.fori_loop(0, share, response_tiles, 0)
    for distance in range(2, levels):
        relay(distance)
        if distance < 4:
            lax.fori_loop((distance - 1) * share, distance * share, response_tiles, 0)
    lax.fori_loop((min(levels, 4) - 1) * share, 4 * share, response_tiles, 0)

    for step in range(1, seqs):
        copy = prefix_copy(step)[1]

        @pl.when(me > 0)
        def _():
            copy.wait_recv()

    @pl.when(me == 0)
    def _():
        for s in range(seqs):
            precv[s] = jnp.zeros((STATE, cb), BF16)

    p_outs = []
    for t in range(2):
        rows = slice(t * TILE, (t + 1) * TILE)
        narrow = pt[2 * t].astype(BF16)
        for s in range(seqs):
            here = slice(s * cb, (s + 1) * cb)
            grown = dot(narrow, pe[0, :, here])
            if t == 1:
                grown = grown * ptot[0, 0:1, here]
            carried = grown * dot(pbc[rows, STATE:], precv[s])
            pout[rows, here] = (pacc[rows, here] + carried).astype(BF16)
        p_outs.append(pltpu.make_async_copy(pout.at[rows], pout_hbm.at[rows], out_sem.at[tiles + t]))
        p_outs[-1].start()

    for level in range(levels):
        which = level * 2 + 1 - core
        pltpu.make_async_remote_copy(
            src_ref=seeds.at[which], dst_ref=seeds.at[which], send_sem=tu_send.at[0], recv_sem=g_recv.at[which],
            device_id={"grp": twin}, device_id_type=MESH).wait_recv()

    def out_copy(tile):
        rows = pl.ds(pl.multiple_of(tile * TILE, TILE), TILE)
        return pltpu.make_async_copy(rout.at[rows], rout_hbm.at[rows], out_sem.at[tile])

    def seeded(tile):
        base = pl.multiple_of(tile * TILE, TILE)
        column = rt[tile]
        owner = column[:, 7 * head_rows + 1 : 7 * head_rows + 2].astype(jnp.int32)
        c_rows = rbc[pl.ds(base + 2 * TILE, TILE), STATE:].astype(F32)
        batch = 8 if grps % 8 == 0 else 2
        total = jnp.zeros((TILE, cb), F32)
        for q in range(0, grps, batch):
            chosen = [jnp.where(owner == q + n, c_rows, 0.0) for n in range(batch)]
            table = seeds[q : q + batch].reshape(batch * STATE, cb)
            total = total + dot(jnp.concatenate(chosen, axis=1).astype(BF16), table)
        result = racc[pl.ds(base, TILE), :] + dot(column.astype(BF16), re[2]) * total
        return jnp.where(owner >= 0, result, 0.0).astype(BF16)

    def seed_tiles(step, carry):
        places = [step * 2 + n for n in range(2)]
        made = [seeded(tile) for tile in places]
        for tile, result in zip(places, made):
            rout[pl.ds(pl.multiple_of(tile * TILE, TILE), TILE), :] = result
            out_copy(tile).start()
        return carry

    lax.fori_loop(0, tiles // 2, seed_tiles, 0)

    for step in range(1, seqs):
        state_copy(step).wait_send()
        peer, copy = prefix_copy(step)

        @pl.when(peer > 0)
        def _():
            copy.wait_send()

    for distance in range(levels):
        @pl.when((z >= distance) & (z < levels - 1))
        def _():
            seed_copy(z - distance, g + 2, up_send.at[distance]).wait_send()

        @pl.when((z + distance < levels) & (z > 0))
        def _():
            seed_copy(z + distance, g - 2, down_send.at[distance]).wait_send()

        @pl.when(z >= distance)
        def _():
            seed_copy(z - distance, twin, tu_send.at[distance]).wait_send()

        if distance > 0:
            @pl.when(z + distance < levels)
            def _():
                seed_copy(z + distance, twin, td_send.at[distance]).wait_send()

    for copy in p_outs:
        copy.wait()

    def out_wait(tile, carry):
        out_copy(tile).wait()
        return carry

    lax.fori_loop(0, tiles, out_wait, 0)


def on_device(
    p_x, p_bc, p_dt, p_decay, r_x, r_bc, r_dt, r_decay, pack_list, resp_len, resp_prompt, d_skip
):
    seqs, grps = lax.axis_size("seq"), lax.axis_size("grp")
    heads = p_dt.shape[1]
    block_heads = heads // seqs
    head_rows = max(8, block_heads)
    slots = pack_list.shape[1]
    tiles = r_x.shape[0] // TILE
    cols, cb = heads * CHANNELS, block_heads * CHANNELS
    if head_rows > block_heads:
        extra = ((0, head_rows - block_heads), (0, 0))
        r_dt, r_decay = jnp.pad(r_dt, extra, constant_values=1.0), jnp.pad(r_decay, extra)
    sizes = (seqs, grps, heads, block_heads, head_rows, slots, tiles)
    levels = grps // 2
    anywhere = pl.BlockSpec(memory_space=pl.ANY)
    dma = pltpu.SemaphoreType.DMA
    p_out, r_out = pl.pallas_call(
        functools.partial(kernel, sizes),
        out_shape=(
            jax.ShapeDtypeStruct((2 * TILE, cols), BF16),
            jax.ShapeDtypeStruct((tiles * TILE, cb), BF16),
        ),
        in_specs=[pl.BlockSpec(memory_space=pltpu.HBM)] * 12,
        out_specs=(anywhere, anywhere),
        scratch_shapes=[
            pltpu.VMEM(p_dt.shape[1:], F32),
            pltpu.VMEM(p_decay.shape[1:], F32),
            pltpu.VMEM(r_dt.shape, F32),
            pltpu.VMEM(r_decay.shape, F32),
            pltpu.SMEM(pack_list.shape, jnp.int32),
            pltpu.SMEM(resp_len.shape, jnp.int32),
            pltpu.SMEM(resp_prompt.shape, jnp.int32),
            pltpu.VMEM((1, heads), F32),
            pltpu.VMEM((tiles, head_rows, TILE), F32),
            pltpu.VMEM((2 * TILE, cols), BF16),
            pltpu.VMEM((2 * TILE, 2 * STATE), BF16),
            pltpu.VMEM((tiles * TILE, cb), BF16),
            pltpu.VMEM(((tiles + 2) * TILE, 2 * STATE), BF16),
            pltpu.VMEM((2, TILE, cols), BF16),
            pltpu.VMEM((4, TILE, TILE), F32),
            pltpu.VMEM((2, TILE, cols), BF16),
            pltpu.VMEM((2, 8, cols), F32),
            pltpu.VMEM((2 * TILE, cols), F32),
            pltpu.VMEM((8, cols), F32),
            pltpu.VMEM((tiles + 2, TILE, cb), BF16),
            pltpu.VMEM((tiles, TILE, TILE), F32),
            pltpu.VMEM((3, TILE, cb), BF16),
            pltpu.VMEM((tiles + 2, 8, cb), F32),
            pltpu.VMEM((tiles * TILE, cb), F32),
            pltpu.VMEM((4 * head_rows, (tiles + 2) * TILE), BF16),
            pltpu.VMEM((seqs, STATE + 16, cb), BF16),
            pltpu.VMEM((seqs, STATE + 16, cb), BF16),
            pltpu.VMEM((seqs, STATE, cb), BF16),
            pltpu.VMEM((seqs, STATE, cb), BF16),
            pltpu.VMEM((grps, STATE, cb), BF16),
            pltpu.VMEM((2 * TILE, cols), BF16),
            pltpu.VMEM((tiles * TILE, cb), BF16),
            dma((12,)),
            dma((tiles + 2,)),
            dma((seqs,)),
            dma((seqs,)),
            dma((seqs,)),
            dma((seqs,)),
            dma((grps,)),
            dma((levels,)),
            dma((levels,)),
            dma((levels,)),
            dma((levels,)),
        ],
        compiler_params=pltpu.CompilerParams(
            collective_id=0, has_side_effects=True, vmem_limit_bytes=63 * 2**20
        ),
        cost_estimate=pl.CostEstimate(flops=4 * 10**9, bytes_accessed=8 * 10**6, transcendentals=4 * 10**6),
        name="scan_and_seeds",
    )(
        p_x[0], p_bc[0], p_dt[0], p_decay[0], r_x, r_bc, r_dt, r_decay,
        pack_list, resp_len, resp_prompt, d_skip[None],
    )
    return p_out[None], r_out


def solution(mesh):
    placed = (
        P("grp", "seq", None),
        P("grp", "seq", None),
        P("grp", None, "seq"),
        P("grp", None, "seq"),
        P("grp", "seq"),
        P("grp", None),
        P("seq", "grp"),
        P("seq", "grp"),
        P("grp", None),
        P(),
        P(),
        P(),
    )
    return jax.shard_map(
        on_device,
        mesh=mesh,
        in_specs=placed,
        out_specs=(P("grp", "seq", None), P("grp", "seq")),
        check_vma=False,
    )
```

```python
import functools

import jax
import jax.numpy as jnp
from jax import lax
from jax.experimental import pallas as pl
from jax.experimental.pallas import tpu as pltpu
from jax.sharding import PartitionSpec as P

TILE = 128
STATE = 128
CHANNELS = 64
LOG2E = 1.4426950408889634
F32 = jnp.float32
BF16 = jnp.bfloat16
MESH = pl.DeviceIdType.MESH


def dot(a, b):
    return jnp.dot(a, b, preferred_element_type=F32)


def dot_nt(a, b):
    return lax.dot_general(a, b, (((1,), (1,)), ((), ())), preferred_element_type=F32)


def dot_tn(a, b):
    return lax.dot_general(a, b, (((0,), (0,)), ((), ())), preferred_element_type=F32)


def split(value, terms):
    parts = []
    for _ in range(terms):
        part = value.astype(BF16).astype(F32)
        parts.append(part)
        value = value - part
    return parts


def iota(shape, dim):
    return lax.broadcasted_iota(jnp.int32, shape, dim)


def spreader(rows, columns, bases):
    row = iota((rows, columns), 0)
    head = iota((rows, columns), 1) >> 6
    hit = row == head + bases[0]
    for base in bases[1:]:
        hit = hit | (row == head + base)
    return jnp.where(hit, 1.0, 0.0).astype(BF16)


def paired(x_pair):
    first = jnp.where(iota(x_pair.shape, 1) < CHANNELS, 1.0, 0.0).astype(BF16)
    second = jnp.where(iota(x_pair.shape, 1) < CHANNELS, 0.0, 1.0).astype(BF16)
    return jnp.concatenate([x_pair * first, x_pair * second], axis=0)


def diagonal(column, row, bias, scores, x_tile, heads):
    pieces = []
    for pair in range(heads // 2):
        mixes = []
        for h in (2 * pair, 2 * pair + 1):
            power = column[:, h : h + 1] + (row[h : h + 1, :] + bias)
            mixes.append((jnp.exp2(power) * scores).astype(BF16))
        x_pair = x_tile[:, pair * 2 * CHANNELS : (pair + 1) * 2 * CHANNELS]
        pieces.append(dot(jnp.concatenate(mixes, axis=1), paired(x_pair)))
    return pieces


def kernel(
    sizes,
    px_hbm, pbc_hbm, pdt_hbm, pdec_hbm, rx_hbm, rbc_hbm, rdt_hbm, rdec_hbm, pack_hbm, len_hbm, prm_hbm, d_hbm,
    pout_hbm, rout_hbm,
    pdt_ref, pdec_ref, rdt, rdec_ref, pack_ref, len_ref, prm_ref, d_ref, rrow, rgrown,
    px, pbc, rx, rbc, pv, pt, pe, ptot, pacc, dwide, rv, rt, re, rtot, racc, rdecs,
    abuf, arecv, pbuf, precv, seeds, pout, rout,
    in_sem, out_sem, a_send, a_recv, x_send, x_recv, g_recv, up_send, down_send, tu_send, td_send,
):
    seqs, grps, heads, block_heads, head_rows, slots, tiles = sizes
    cols = heads * CHANNELS
    cb = block_heads * CHANNELS
    me = lax.axis_index("seq")
    g = lax.axis_index("grp")
    z, core = g // 2, lax.rem(g, 2)
    levels = grps // 2
    twin = z * 2 + 1 - core

    loads = [
        pltpu.make_async_copy(px_hbm, px, in_sem.at[0]),
        pltpu.make_async_copy(pbc_hbm, pbc, in_sem.at[1]),
        pltpu.make_async_copy(rx_hbm, rx, in_sem.at[2]),
        pltpu.make_async_copy(rbc_hbm, rbc.at[pl.ds(2 * TILE, tiles * TILE)], in_sem.at[3]),
    ]
    small = [(pdec_hbm, pdec_ref), (pdt_hbm, pdt_ref), (d_hbm, d_ref), (pack_hbm, pack_ref), (len_hbm, len_ref),
             (prm_hbm, prm_ref), (rdec_hbm, rdec_ref), (rdt_hbm, rdt)]
    loads += [pltpu.make_async_copy(src, dst, in_sem.at[4 + n]) for n, (src, dst) in enumerate(small)]
    for n in (4, 5, 0, 1, 6, 7, 8, 9, 10, 11, 2, 3):
        loads[n].start()

    barrier = pltpu.get_barrier_semaphore()
    for step in range(1, seqs):
        pl.semaphore_signal(barrier, inc=1, device_id={"seq": lax.rem(me + step, seqs)}, device_id_type=MESH)
    pl.semaphore_signal(barrier, inc=1, device_id={"grp": twin}, device_id_type=MESH)

    @pl.when(z > 0)
    def _():
        pl.semaphore_signal(barrier, inc=1, device_id={"grp": g - 2}, device_id_type=MESH)

    @pl.when(z < levels - 1)
    def _():
        pl.semaphore_signal(barrier, inc=1, device_id={"grp": g + 2}, device_id_type=MESH)

    each = spreader(heads, cols, (0,))
    none = jnp.zeros((heads, cols), BF16)
    pe[0] = jnp.concatenate([none, each, each, none], axis=0)
    pe[1] = jnp.concatenate([each, each, none, none], axis=0)
    re[0] = spreader(TILE, cb, (head_rows, 2 * head_rows))
    re[1] = spreader(TILE, cb, (3 * head_rows, 4 * head_rows))
    re[2] = spreader(TILE, cb, (5 * head_rows, 6 * head_rows))
    for n in (4, 5, 6):
        loads[n].wait()
    row8 = iota((8, heads), 0)
    skips = split(jnp.broadcast_to(d_ref[...], (8, heads)), 3)
    skip_rows = jnp.where(row8 == 0, skips[0], jnp.where(row8 == 1, skips[1], jnp.where(row8 == 2, skips[2], 0.0)))
    skip_wide = dot(skip_rows.astype(BF16), each)
    dwide[...] = jnp.broadcast_to(jnp.sum(skip_wide, axis=0, keepdims=True), (8, cols))

    before = iota((TILE, TILE), 0) <= iota((TILE, TILE), 1)
    upper = jnp.where(before, 1.0, 0.0).astype(BF16)
    low_bias = jnp.where(iota((TILE, TILE), 1) <= iota((TILE, TILE), 0), 0.0, -1e30)

    prow = []
    for t in range(2):
        lanes = slice(t * TILE, (t + 1) * TILE)
        parts = split(pdec_ref[:, lanes], 3)
        sums = dot(jnp.concatenate(parts, axis=0).astype(BF16), upper)
        cum = sums[:heads] + sums[heads : 2 * heads] + sums[2 * heads :]
        dt = pdt_ref[:, lanes]
        c2 = cum * LOG2E
        prow.append(jnp.log2(dt) - c2)
        grown = split(jnp.exp2(c2), 2)
        weight = split(jnp.exp2(c2[:, TILE - 1 :] - c2) * dt, 2)
        fill = jnp.zeros((TILE - 3 * heads, TILE), F32)
        pt[2 * t] = jnp.concatenate([c2] + grown + [fill], axis=0).T
        fill = jnp.zeros((TILE - 2 * heads, TILE), F32)
        pt[2 * t + 1] = jnp.concatenate(weight + [fill], axis=0).T
    loads[0].wait()
    loads[1].wait()
    chunk = min(cols, 512)
    weights = jnp.concatenate([pt[1], pt[3]], axis=0).astype(BF16)
    lasts = jnp.concatenate([pt[0, TILE - 8 :, :], pt[2, TILE - 8 :, :]], axis=0).astype(BF16)
    for start in range(0, cols, chunk):
        here = slice(start, start + chunk)
        scaled = (px[:, here].astype(F32) * dot(weights, pe[1, :, here])).astype(BF16)
        last = dot(lasts, pe[0, :, here])
        for t in range(2):
            pv[t, :, here] = scaled[t * TILE : (t + 1) * TILE]
            ptot[t, :, here] = jnp.broadcast_to(last[8 * t + 7 : 8 * t + 8], (8, chunk))
    for s in range(seqs):
        here = slice(s * cb, (s + 1) * cb)
        t0, t1 = ptot[0, 0:1, here], ptot[1, 0:1, here]
        ended = t1 * dot_tn(pbc[0:TILE, :STATE], pv[0, :, here]) + dot_tn(pbc[TILE:, :STATE], pv[1, :, here])
        abuf[s, 0:STATE, :] = ended.astype(BF16)
        hi, lo = split(t0 * t1, 2)
        row = iota((16, cb), 0)
        abuf[s, STATE:, :] = jnp.where(row == 0, hi, jnp.where(row == 1, lo, 0.0)).astype(BF16)

    pl.semaphore_wait(barrier, seqs + jnp.where(z > 0, 1, 0) + jnp.where(z < levels - 1, 1, 0))

    def state_copy(step):
        peer = lax.rem(me + step, seqs)
        return pltpu.make_async_remote_copy(
            src_ref=abuf.at[peer], dst_ref=arecv.at[me], send_sem=a_send.at[step], recv_sem=a_recv.at[step],
            device_id={"seq": peer}, device_id_type=MESH)

    def prefix_copy(step):
        peer = lax.rem(me + step, seqs)
        return peer, pltpu.make_async_remote_copy(
            src_ref=pbuf.at[peer], dst_ref=precv.at[me], send_sem=x_send.at[step], recv_sem=x_recv.at[step],
            device_id={"seq": peer}, device_id_type=MESH)

    def seed_copy(level, target, send_sem):
        which = level * 2 + core
        return pltpu.make_async_remote_copy(
            src_ref=seeds.at[which], dst_ref=seeds.at[which], send_sem=send_sem, recv_sem=g_recv.at[which],
            device_id={"grp": target}, device_id_type=MESH)

    for step in range(1, seqs):
        state_copy(step).start()
    arecv[me] = abuf[me]

    for t in range(2):
        rows = slice(t * TILE, (t + 1) * TILE)
        b_rows, c_rows = pbc[rows, :STATE], pbc[rows, STATE:]
        scores = dot_nt(c_rows, b_rows)
        column = pt[2 * t]
        x_tile = px[rows, :]
        pieces = diagonal(column, prow[t], low_bias, scores, x_tile, heads)
        for pair, piece in enumerate(pieces):
            here = slice(pair * 2 * CHANNELS, (pair + 1) * 2 * CHANNELS)
            pacc[rows, here] = piece + dwide[0:1, here] * x_tile[:, here].astype(F32)
        if t == 1:
            cross = dot_nt(c_rows, pbc[0:TILE, :STATE]).astype(BF16)
            for start in range(0, cols, chunk):
                here = slice(start, start + chunk)
                grown = dot(column.astype(BF16), pe[0, :, here])
                pacc[rows, here] += grown * dot(cross, pv[0, :, here])

    for step in range(1, seqs):
        state_copy(step).wait_recv()
    ahead = jnp.zeros((STATE, cb), F32)
    for s in range(seqs):
        pbuf[s] = ahead.astype(BF16)
        decay = arecv[s, STATE:, :].astype(F32)
        ahead = (decay[0:1] + decay[1:2]) * ahead + arecv[s, 0:STATE, :].astype(F32)
    seeds[g] = ahead.astype(BF16)

    def pass_on(level, distance, up):
        if up:
            @pl.when(z < levels - 1)
            def _():
                seed_copy(level, g + 2, up_send.at[distance]).start()
        else:
            @pl.when(z > 0)
            def _():
                seed_copy(level, g - 2, down_send.at[distance]).start()

    pass_on(z, 0, True)
    pass_on(z, 0, False)
    seed_copy(z, twin, tu_send.at[0]).start()
    for step in range(1, seqs):
        peer, copy = prefix_copy(step)

        @pl.when(peer > 0)
        def _():
            copy.start()

    precv[me] = pbuf[me]

    for n in range(7, 12):
        loads[n].wait()
    limits, owners, edge = [], [], jnp.int32(0)
    for k in range(slots):
        which = pack_ref[0, k]
        there = which >= 0
        which = jnp.maximum(which, 0)
        owners.append(jnp.where(there, prm_ref[which], -1))
        limits.append(edge)
        edge = edge + jnp.where(there, len_ref[which], 0)
    limits.append(edge)

    rbc[0 : 2 * TILE, :] = jnp.zeros((2 * TILE, 2 * STATE), BF16)
    rv[0:2] = jnp.zeros((2, TILE, cb), BF16)
    rtot[0:2] = jnp.zeros((2, 8, cb), F32)
    parts = split(rdec_ref[...], 3)
    rdecs[:, 0 : 2 * TILE] = jnp.zeros((4 * head_rows, 2 * TILE), BF16)
    rdecs[:, 2 * TILE :] = jnp.concatenate(parts + [jnp.zeros_like(parts[0])], axis=0).astype(BF16)
    my_cols = pl.ds(pl.multiple_of(me * cb, cb), cb)
    loads[2].wait()
    loads[3].wait()

    def prepare(tile):
        base = pl.multiple_of(tile * TILE, TILE)
        rows = pl.ds(base, TILE)
        place = base + iota((8, TILE), 1)
        start = jnp.zeros((8, TILE), jnp.int32)
        owner = jnp.full((8, TILE), -1, jnp.int32)
        for k in range(slots):
            start = jnp.where(place >= limits[k], limits[k], start)
            owner = jnp.where((place >= limits[k]) & (place < limits[k + 1]), owners[k], owner)
        start = jnp.where(place >= limits[slots], limits[slots], start) - base

        j = iota((3 * TILE, TILE), 0) - 2 * TILE
        i = iota((3 * TILE, TILE), 1)
        ordered = j <= i
        in_slot = jnp.where(ordered & (j >= start[0:1]), 1.0, 0.0)
        in_tile = jnp.where(ordered & (j >= 0), 1.0, 0.0)
        sums = dot(rdecs[:, pl.ds(base, 3 * TILE)], jnp.concatenate([in_slot, in_tile], axis=1).astype(BF16))
        sums = sums[:head_rows] + sums[head_rows : 2 * head_rows] + sums[2 * head_rows : 3 * head_rows]
        gain, c2 = sums[:, :TILE] * LOG2E, sums[:, TILE:] * LOG2E
        dt = rdt[:, rows]
        where_rows = jnp.where(iota((8, TILE), 0) == 0, start, owner).astype(F32)
        stack = [c2] + split(jnp.exp2(c2), 2) + split(jnp.exp2(c2[:, TILE - 1 :] - c2) * dt, 2)
        stack += split(jnp.exp2(gain), 2) + [where_rows]
        stack += [jnp.zeros((TILE - 7 * head_rows - 8, TILE), F32)]
        column = jnp.concatenate(stack, axis=0).T
        return column, jnp.log2(dt) - c2

    def prepare_some(step, carry):
        base = pl.multiple_of(step * together * TILE, TILE)
        rows = pl.ds(base, together * TILE)
        made = [prepare(step * together + n) for n in range(together)]
        narrow = jnp.concatenate([column for column, _ in made], axis=0).astype(BF16)
        wide = dot(narrow, re[1])
        grown = dot(narrow, re[0])
        scaled = (rx[rows, :].astype(F32) * wide).astype(BF16)
        rgrown[rows, :] = grown
        rv[pl.ds(step * together + 2, together)] = scaled.reshape(together, TILE, cb)
        for n, (column, row_form) in enumerate(made):
            tile = step * together + n
            rt[tile] = column
            rrow[tile] = row_form
            rtot[tile + 2] = jnp.broadcast_to(grown[(n + 1) * TILE - 1 : (n + 1) * TILE], (8, cb))
        return carry

    def within(tile):
        base = pl.multiple_of(tile * TILE, TILE)
        rows = pl.ds(base, TILE)
        column = rt[tile]
        x_tile = rx[rows, :]
        grown = rgrown[rows, :]
        c_rows = rbc[pl.ds(base + 2 * TILE, TILE), STATE:]
        scores = dot_nt(c_rows, rbc[pl.ds(base, 3 * TILE), :STATE])
        j = iota((TILE, 3 * TILE), 1) - 2 * TILE
        first = column[:, 7 * head_rows : 7 * head_rows + 1].astype(jnp.int32)
        seen = (j <= iota((TILE, 3 * TILE), 0)) & (j >= first)
        bias = jnp.where(seen[:, 2 * TILE :], 0.0, -1e30)
        cross = jnp.where(seen[:, : 2 * TILE], scores[:, : 2 * TILE], 0.0).astype(BF16)
        earlier = dot(cross[:, TILE:], rv[tile + 1]) + rtot[tile + 1, 0:1] * dot(cross[:, :TILE], rv[tile])
        pieces = diagonal(column, rrow[tile], bias, scores[:, 2 * TILE :], x_tile, block_heads)
        skip = dwide[0:1, my_cols]
        return jnp.concatenate(pieces, axis=1) + grown * earlier + skip * x_tile.astype(F32)

    def response_tiles(step, carry):
        places = [step * 2 + n for n in range(2)]
        made = [within(tile) for tile in places]
        for tile, total in zip(places, made):
            racc[pl.ds(pl.multiple_of(tile * TILE, TILE), TILE), :] = total
        return carry

    def relay(distance):
        @pl.when(z >= distance)
        def _():
            seed_copy(z - distance, twin, tu_send.at[distance]).wait_recv()
            pass_on(z - distance, distance, True)
            seed_copy(z - distance, twin, tu_send.at[distance]).start()

        @pl.when(z + distance < levels)
        def _():
            seed_copy(z + distance, twin, td_send.at[distance]).wait_recv()
            pass_on(z + distance, distance, False)
            seed_copy(z + distance, twin, td_send.at[distance]).start()

    together = 4
    share = tiles // 8
    lax.fori_loop(0, tiles // together, prepare_some, 0)
    relay(1)
    lax.fori_loop(0, share, response_tiles, 0)
    for distance in range(2, levels):
        relay(distance)
        if distance < 4:
            lax.fori_loop((distance - 1) * share, distance * share, response_tiles, 0)
    lax.fori_loop((min(levels, 4) - 1) * share, 4 * share, response_tiles, 0)

    for step in range(1, seqs):
        copy = prefix_copy(step)[1]

        @pl.when(me > 0)
        def _():
            copy.wait_recv()

    @pl.when(me == 0)
    def _():
        for s in range(seqs):
            precv[s] = jnp.zeros((STATE, cb), BF16)

    narrow = jnp.concatenate([pt[0], pt[2]], axis=0).astype(BF16)
    later = iota((2 * TILE, cb), 0) >= TILE
    for s in range(seqs):
        here = slice(s * cb, (s + 1) * cb)
        grown = dot(narrow, pe[0, :, here]) * jnp.where(later, ptot[0, 0:1, here], 1.0)
        carried = grown * dot(pbc[:, STATE:], precv[s])
        pout[:, here] = (pacc[:, here] + carried).astype(BF16)
    p_outs = [pltpu.make_async_copy(pout, pout_hbm, out_sem.at[tiles])]
    p_outs[0].start()

    for level in range(levels):
        which = level * 2 + 1 - core
        pltpu.make_async_remote_copy(
            src_ref=seeds.at[which], dst_ref=seeds.at[which], send_sem=tu_send.at[0], recv_sem=g_recv.at[which],
            device_id={"grp": twin}, device_id_type=MESH).wait_recv()

    def out_copy(step):
        rows = pl.ds(pl.multiple_of(step * together * TILE, TILE), together * TILE)
        return pltpu.make_async_copy(rout.at[rows], rout_hbm.at[rows], out_sem.at[step])

    def seed_tiles(step, carry):
        base = pl.multiple_of(step * together * TILE, TILE)
        rows = pl.ds(base, together * TILE)
        column = rt[pl.ds(step * together, together)].reshape(together * TILE, TILE)
        owner = column[:, 7 * head_rows + 1 : 7 * head_rows + 2].astype(jnp.int32)
        c_rows = rbc[pl.ds(base + 2 * TILE, together * TILE), STATE:].astype(F32)
        batch = 8 if grps % 8 == 0 else 2
        total = jnp.zeros((together * TILE, cb), F32)
        for q in range(0, grps, batch):
            chosen = [jnp.where(owner == q + n, c_rows, 0.0).astype(BF16) for n in range(batch)]
            table = seeds[q : q + batch].reshape(batch * STATE, cb)
            total = total + dot(jnp.concatenate(chosen, axis=1), table)
        result = racc[rows, :] + dot(column.astype(BF16), re[2]) * total
        rout[rows, :] = jnp.where(owner >= 0, result, 0.0).astype(BF16)
        out_copy(step).start()
        return carry

    lax.fori_loop(0, tiles // together, seed_tiles, 0)

    for step in range(1, seqs):
        state_copy(step).wait_send()
        peer, copy = prefix_copy(step)

        @pl.when(peer > 0)
        def _():
            copy.wait_send()

    for distance in range(levels):
        @pl.when((z >= distance) & (z < levels - 1))
        def _():
            seed_copy(z - distance, g + 2, up_send.at[distance]).wait_send()

        @pl.when((z + distance < levels) & (z > 0))
        def _():
            seed_copy(z + distance, g - 2, down_send.at[distance]).wait_send()

        @pl.when(z >= distance)
        def _():
            seed_copy(z - distance, twin, tu_send.at[distance]).wait_send()

        if distance > 0:
            @pl.when(z + distance < levels)
            def _():
                seed_copy(z + distance, twin, td_send.at[distance]).wait_send()

    for copy in p_outs:
        copy.wait()

    def out_wait(step, carry):
        out_copy(step).wait()
        return carry

    lax.fori_loop(0, tiles // together, out_wait, 0)


def on_device(
    p_x, p_bc, p_dt, p_decay, r_x, r_bc, r_dt, r_decay, pack_list, resp_len, resp_prompt, d_skip
):
    seqs, grps = lax.axis_size("seq"), lax.axis_size("grp")
    heads = p_dt.shape[1]
    block_heads = heads // seqs
    head_rows = max(8, block_heads)
    slots = pack_list.shape[1]
    tiles = r_x.shape[0] // TILE
    cols, cb = heads * CHANNELS, block_heads * CHANNELS
    if head_rows > block_heads:
        extra = ((0, head_rows - block_heads), (0, 0))
        r_dt, r_decay = jnp.pad(r_dt, extra, constant_values=1.0), jnp.pad(r_decay, extra)
    sizes = (seqs, grps, heads, block_heads, head_rows, slots, tiles)
    levels = grps // 2
    anywhere = pl.BlockSpec(memory_space=pl.ANY)
    dma = pltpu.SemaphoreType.DMA
    p_out, r_out = pl.pallas_call(
        functools.partial(kernel, sizes),
        out_shape=(
            jax.ShapeDtypeStruct((2 * TILE, cols), BF16),
            jax.ShapeDtypeStruct((tiles * TILE, cb), BF16),
        ),
        in_specs=[pl.BlockSpec(memory_space=pltpu.HBM)] * 12,
        out_specs=(anywhere, anywhere),
        scratch_shapes=[
            pltpu.VMEM(p_dt.shape[1:], F32),
            pltpu.VMEM(p_decay.shape[1:], F32),
            pltpu.VMEM(r_dt.shape, F32),
            pltpu.VMEM(r_decay.shape, F32),
            pltpu.SMEM(pack_list.shape, jnp.int32),
            pltpu.SMEM(resp_len.shape, jnp.int32),
            pltpu.SMEM(resp_prompt.shape, jnp.int32),
            pltpu.VMEM((1, heads), F32),
            pltpu.VMEM((tiles, head_rows, TILE), F32),
            pltpu.VMEM((tiles * TILE, cb), F32),
            pltpu.VMEM((2 * TILE, cols), BF16),
            pltpu.VMEM((2 * TILE, 2 * STATE), BF16),
            pltpu.VMEM((tiles * TILE, cb), BF16),
            pltpu.VMEM(((tiles + 2) * TILE, 2 * STATE), BF16),
            pltpu.VMEM((2, TILE, cols), BF16),
            pltpu.VMEM((4, TILE, TILE), F32),
            pltpu.VMEM((2, TILE, cols), BF16),
            pltpu.VMEM((2, 8, cols), F32),
            pltpu.VMEM((2 * TILE, cols), F32),
            pltpu.VMEM((8, cols), F32),
            pltpu.VMEM((tiles + 2, TILE, cb), BF16),
            pltpu.VMEM((tiles, TILE, TILE), F32),
            pltpu.VMEM((3, TILE, cb), BF16),
            pltpu.VMEM((tiles + 2, 8, cb), F32),
            pltpu.VMEM((tiles * TILE, cb), F32),
            pltpu.VMEM((4 * head_rows, (tiles + 2) * TILE), BF16),
            pltpu.VMEM((seqs, STATE + 16, cb), BF16),
            pltpu.VMEM((seqs, STATE + 16, cb), BF16),
            pltpu.VMEM((seqs, STATE, cb), BF16),
            pltpu.VMEM((seqs, STATE, cb), BF16),
            pltpu.VMEM((grps, STATE, cb), BF16),
            pltpu.VMEM((2 * TILE, cols), BF16),
            pltpu.VMEM((tiles * TILE, cb), BF16),
            dma((12,)),
            dma((tiles + 2,)),
            dma((seqs,)),
            dma((seqs,)),
            dma((seqs,)),
            dma((seqs,)),
            dma((grps,)),
            dma((levels,)),
            dma((levels,)),
            dma((levels,)),
            dma((levels,)),
        ],
        compiler_params=pltpu.CompilerParams(
            collective_id=0, has_side_effects=True, vmem_limit_bytes=63 * 2**20
        ),
        cost_estimate=pl.CostEstimate(flops=4 * 10**9, bytes_accessed=8 * 10**6, transcendentals=4 * 10**6),
        name="scan_and_seeds",
    )(
        p_x[0], p_bc[0], p_dt[0], p_decay[0], r_x, r_bc, r_dt, r_decay,
        pack_list, resp_len, resp_prompt, d_skip[None],
    )
    return p_out[None], r_out


def solution(mesh):
    placed = (
        P("grp", "seq", None),
        P("grp", "seq", None),
        P("grp", None, "seq"),
        P("grp", None, "seq"),
        P("grp", "seq"),
        P("grp", None),
        P("seq", "grp"),
        P("seq", "grp"),
        P("grp", None),
        P(),
        P(),
        P(),
    )
    return jax.shard_map(
        on_device,
        mesh=mesh,
        in_specs=placed,
        out_specs=(P("grp", "seq", None), P("grp", "seq")),
        check_vma=False,
    )
```

```python
import functools

import jax
import jax.numpy as jnp
from jax import lax
from jax.experimental import pallas as pl
from jax.experimental.pallas import tpu as pltpu
from jax.sharding import PartitionSpec as P

TILE = 128
STATE = 128
CHANNELS = 64
LOG2E = 1.4426950408889634
F32 = jnp.float32
BF16 = jnp.bfloat16
MESH = pl.DeviceIdType.MESH


def dot(a, b):
    return jnp.dot(a, b, preferred_element_type=F32)


def dot_nt(a, b):
    return lax.dot_general(a, b, (((1,), (1,)), ((), ())), preferred_element_type=F32)


def dot_tn(a, b):
    return lax.dot_general(a, b, (((0,), (0,)), ((), ())), preferred_element_type=F32)


def split(value, terms):
    parts = []
    for _ in range(terms):
        part = value.astype(BF16).astype(F32)
        parts.append(part)
        value = value - part
    return parts


def iota(shape, dim):
    return lax.broadcasted_iota(jnp.int32, shape, dim)


def spreader(rows, columns, bases):
    row = iota((rows, columns), 0)
    head = iota((rows, columns), 1) >> 6
    hit = row == head + bases[0]
    for base in bases[1:]:
        hit = hit | (row == head + base)
    return jnp.where(hit, 1.0, 0.0).astype(BF16)


def paired(x_pair):
    first = jnp.where(iota(x_pair.shape, 1) < CHANNELS, 1.0, 0.0).astype(BF16)
    second = jnp.where(iota(x_pair.shape, 1) < CHANNELS, 0.0, 1.0).astype(BF16)
    return jnp.concatenate([x_pair * first, x_pair * second], axis=0)


def diagonal(column, row, bias, scores, x_tile, heads):
    pieces = []
    for pair in range(heads // 2):
        mixes = []
        for h in (2 * pair, 2 * pair + 1):
            power = column[:, h : h + 1] + (row[h : h + 1, :] + bias)
            mixes.append((jnp.exp2(power) * scores).astype(BF16))
        x_pair = x_tile[:, pair * 2 * CHANNELS : (pair + 1) * 2 * CHANNELS]
        pieces.append(dot(jnp.concatenate(mixes, axis=1), paired(x_pair)))
    return pieces


def kernel(
    sizes,
    px_hbm, pbc_hbm, pdt_hbm, pdec_hbm, rx_hbm, rbc_hbm, rdt_hbm, rdec_hbm, pack_hbm, len_hbm, prm_hbm, d_hbm,
    pout_hbm, rout_hbm,
    pdt_ref, pdec_ref, rdt, rdec_ref, pack_ref, len_ref, prm_ref, d_ref, rrow, rgrown,
    px, pbc, rx, rbc, pv, pt, pe, ptot, pacc, dwide, rv, rt, re, rtot, racc, rdecs,
    abuf, arecv, pbuf, precv, seeds, pout, rout,
    in_sem, out_sem, a_send, a_recv, x_send, x_recv, g_recv, up_send, down_send, tu_send, td_send,
):
    seqs, grps, heads, block_heads, head_rows, slots, tiles = sizes
    cols = heads * CHANNELS
    cb = block_heads * CHANNELS
    me = lax.axis_index("seq")
    g = lax.axis_index("grp")
    z, core = g // 2, lax.rem(g, 2)
    levels = grps // 2
    twin = z * 2 + 1 - core

    loads = [
        pltpu.make_async_copy(px_hbm, px, in_sem.at[0]),
        pltpu.make_async_copy(pbc_hbm, pbc, in_sem.at[1]),
        pltpu.make_async_copy(rx_hbm, rx, in_sem.at[2]),
        pltpu.make_async_copy(rbc_hbm, rbc.at[pl.ds(2 * TILE, tiles * TILE)], in_sem.at[3]),
    ]
    small = [(pdec_hbm, pdec_ref), (pdt_hbm, pdt_ref), (d_hbm, d_ref), (pack_hbm, pack_ref), (len_hbm, len_ref),
             (prm_hbm, prm_ref), (rdec_hbm, rdec_ref), (rdt_hbm, rdt)]
    loads += [pltpu.make_async_copy(src, dst, in_sem.at[4 + n]) for n, (src, dst) in enumerate(small)]
    for n in (4, 5, 0, 1, 6, 7, 8, 9, 10, 11, 2, 3):
        loads[n].start()

    barrier = pltpu.get_barrier_semaphore()
    for step in range(1, seqs):
        pl.semaphore_signal(barrier, inc=1, device_id={"seq": lax.rem(me + step, seqs)}, device_id_type=MESH)
    pl.semaphore_signal(barrier, inc=1, device_id={"grp": twin}, device_id_type=MESH)

    @pl.when(z > 0)
    def _():
        pl.semaphore_signal(barrier, inc=1, device_id={"grp": g - 2}, device_id_type=MESH)

    @pl.when(z < levels - 1)
    def _():
        pl.semaphore_signal(barrier, inc=1, device_id={"grp": g + 2}, device_id_type=MESH)

    each = spreader(heads, cols, (0,))
    none = jnp.zeros((heads, cols), BF16)
    pe[0] = jnp.concatenate([none, each, each, none], axis=0)
    pe[1] = jnp.concatenate([each, each, none, none], axis=0)
    re[0] = spreader(TILE, cb, (head_rows, 2 * head_rows))
    re[1] = spreader(TILE, cb, (3 * head_rows, 4 * head_rows))
    re[2] = spreader(TILE, cb, (5 * head_rows, 6 * head_rows))
    for n in (4, 5, 6):
        loads[n].wait()
    row8 = iota((8, heads), 0)
    skips = split(jnp.broadcast_to(d_ref[...], (8, heads)), 3)
    skip_rows = jnp.where(row8 == 0, skips[0], jnp.where(row8 == 1, skips[1], jnp.where(row8 == 2, skips[2], 0.0)))
    skip_wide = dot(skip_rows.astype(BF16), each)
    dwide[...] = jnp.broadcast_to(jnp.sum(skip_wide, axis=0, keepdims=True), (8, cols))

    before = iota((TILE, TILE), 0) <= iota((TILE, TILE), 1)
    upper = jnp.where(before, 1.0, 0.0).astype(BF16)
    low_bias = jnp.where(iota((TILE, TILE), 1) <= iota((TILE, TILE), 0), 0.0, -1e30)

    prow = []
    for t in range(2):
        lanes = slice(t * TILE, (t + 1) * TILE)
        parts = split(pdec_ref[:, lanes], 3)
        sums = dot(jnp.concatenate(parts, axis=0).astype(BF16), upper)
        cum = sums[:heads] + sums[heads : 2 * heads] + sums[2 * heads :]
        dt = pdt_ref[:, lanes]
        c2 = cum * LOG2E
        prow.append(jnp.log2(dt) - c2)
        grown = split(jnp.exp2(c2), 2)
        weight = split(jnp.exp2(c2[:, TILE - 1 :] - c2) * dt, 2)
        fill = jnp.zeros((TILE - 3 * heads, TILE), F32)
        pt[2 * t] = jnp.concatenate([c2] + grown + [fill], axis=0).T
        fill = jnp.zeros((TILE - 2 * heads, TILE), F32)
        pt[2 * t + 1] = jnp.concatenate(weight + [fill], axis=0).T
    loads[0].wait()
    loads[1].wait()
    chunk = min(cols, 512)
    weights = jnp.concatenate([pt[1], pt[3]], axis=0).astype(BF16)
    lasts = jnp.concatenate([pt[0, TILE - 8 :, :], pt[2, TILE - 8 :, :]], axis=0).astype(BF16)
    for start in range(0, cols, chunk):
        here = slice(start, start + chunk)
        scaled = (px[:, here].astype(F32) * dot(weights, pe[1, :, here])).astype(BF16)
        last = dot(lasts, pe[0, :, here])
        for t in range(2):
            pv[t, :, here] = scaled[t * TILE : (t + 1) * TILE]
            ptot[t, :, here] = jnp.broadcast_to(last[8 * t + 7 : 8 * t + 8], (8, chunk))
    for s in range(seqs):
        here = slice(s * cb, (s + 1) * cb)
        t0, t1 = ptot[0, 0:1, here], ptot[1, 0:1, here]
        ended = t1 * dot_tn(pbc[0:TILE, :STATE], pv[0, :, here]) + dot_tn(pbc[TILE:, :STATE], pv[1, :, here])
        abuf[s, 0:STATE, :] = ended.astype(BF16)
        hi, lo = split(t0 * t1, 2)
        row = iota((16, cb), 0)
        abuf[s, STATE:, :] = jnp.where(row == 0, hi, jnp.where(row == 1, lo, 0.0)).astype(BF16)

    pl.semaphore_wait(barrier, seqs + jnp.where(z > 0, 1, 0) + jnp.where(z < levels - 1, 1, 0))

    def state_copy(step):
        peer = lax.rem(me + step, seqs)
        return pltpu.make_async_remote_copy(
            src_ref=abuf.at[peer], dst_ref=arecv.at[me], send_sem=a_send.at[step], recv_sem=a_recv.at[step],
            device_id={"seq": peer}, device_id_type=MESH)

    def prefix_copy(step):
        peer = lax.rem(me + step, seqs)
        return peer, pltpu.make_async_remote_copy(
            src_ref=pbuf.at[peer], dst_ref=precv.at[me], send_sem=x_send.at[step], recv_sem=x_recv.at[step],
            device_id={"seq": peer}, device_id_type=MESH)

    def seed_copy(level, target, send_sem):
        which = level * 2 + core
        return pltpu.make_async_remote_copy(
            src_ref=seeds.at[which], dst_ref=seeds.at[which], send_sem=send_sem, recv_sem=g_recv.at[which],
            device_id={"grp": target}, device_id_type=MESH)

    for step in range(1, seqs):
        state_copy(step).start()
    arecv[me] = abuf[me]

    for t in range(2):
        rows = slice(t * TILE, (t + 1) * TILE)
        b_rows, c_rows = pbc[rows, :STATE], pbc[rows, STATE:]
        scores = dot_nt(c_rows, b_rows)
        column = pt[2 * t]
        x_tile = px[rows, :]
        pieces = diagonal(column, prow[t], low_bias, scores, x_tile, heads)
        for pair, piece in enumerate(pieces):
            here = slice(pair * 2 * CHANNELS, (pair + 1) * 2 * CHANNELS)
            pacc[rows, here] = piece + dwide[0:1, here] * x_tile[:, here].astype(F32)
        if t == 1:
            cross = dot_nt(c_rows, pbc[0:TILE, :STATE]).astype(BF16)
            for start in range(0, cols, chunk):
                here = slice(start, start + chunk)
                grown = dot(column.astype(BF16), pe[0, :, here])
                pacc[rows, here] += grown * dot(cross, pv[0, :, here])

    for step in range(1, seqs):
        state_copy(step).wait_recv()
    ahead = jnp.zeros((STATE, cb), F32)
    for s in range(seqs):
        pbuf[s] = ahead.astype(BF16)
        decay = arecv[s, STATE:, :].astype(F32)
        ahead = (decay[0:1] + decay[1:2]) * ahead + arecv[s, 0:STATE, :].astype(F32)
    seeds[g] = ahead.astype(BF16)

    def pass_on(level, distance, up):
        if up:
            @pl.when(z < levels - 1)
            def _():
                seed_copy(level, g + 2, up_send.at[distance]).start()
        else:
            @pl.when(z > 0)
            def _():
                seed_copy(level, g - 2, down_send.at[distance]).start()

    pass_on(z, 0, True)
    pass_on(z, 0, False)
    seed_copy(z, twin, tu_send.at[0]).start()
    for step in range(1, seqs):
        peer, copy = prefix_copy(step)

        @pl.when(peer > 0)
        def _():
            copy.start()

    precv[me] = pbuf[me]

    for n in range(7, 12):
        loads[n].wait()
    limits, owners, edge = [], [], jnp.int32(0)
    for k in range(slots):
        which = pack_ref[0, k]
        there = which >= 0
        which = jnp.maximum(which, 0)
        owners.append(jnp.where(there, prm_ref[which], -1))
        limits.append(edge)
        edge = edge + jnp.where(there, len_ref[which], 0)
    limits.append(edge)

    rbc[0 : 2 * TILE, :] = jnp.zeros((2 * TILE, 2 * STATE), BF16)
    rv[0:2] = jnp.zeros((2, TILE, cb), BF16)
    rtot[0:2] = jnp.zeros((2, 8, cb), F32)
    parts = split(rdec_ref[...], 3)
    rdecs[:, 0 : 2 * TILE] = jnp.zeros((4 * head_rows, 2 * TILE), BF16)
    rdecs[:, 2 * TILE :] = jnp.concatenate(parts + [jnp.zeros_like(parts[0])], axis=0).astype(BF16)
    my_cols = pl.ds(pl.multiple_of(me * cb, cb), cb)
    loads[2].wait()
    loads[3].wait()

    def prepare(tile):
        base = pl.multiple_of(tile * TILE, TILE)
        rows = pl.ds(base, TILE)
        place = base + iota((8, TILE), 1)
        start = jnp.zeros((8, TILE), jnp.int32)
        owner = jnp.full((8, TILE), -1, jnp.int32)
        for k in range(slots):
            start = jnp.where(place >= limits[k], limits[k], start)
            owner = jnp.where((place >= limits[k]) & (place < limits[k + 1]), owners[k], owner)
        start = jnp.where(place >= limits[slots], limits[slots], start) - base

        j = iota((3 * TILE, TILE), 0) - 2 * TILE
        i = iota((3 * TILE, TILE), 1)
        ordered = j <= i
        in_slot = jnp.where(ordered & (j >= start[0:1]), 1.0, 0.0)
        in_tile = jnp.where(ordered & (j >= 0), 1.0, 0.0)
        sums = dot(rdecs[:, pl.ds(base, 3 * TILE)], jnp.concatenate([in_slot, in_tile], axis=1).astype(BF16))
        sums = sums[:head_rows] + sums[head_rows : 2 * head_rows] + sums[2 * head_rows : 3 * head_rows]
        gain, c2 = sums[:, :TILE] * LOG2E, sums[:, TILE:] * LOG2E
        dt = rdt[:, rows]
        where_rows = jnp.where(iota((8, TILE), 0) == 0, start, owner).astype(F32)
        stack = [c2] + split(jnp.exp2(c2), 2) + split(jnp.exp2(c2[:, TILE - 1 :] - c2) * dt, 2)
        stack += split(jnp.exp2(gain), 2) + [where_rows]
        stack += [jnp.zeros((TILE - 7 * head_rows - 8, TILE), F32)]
        column = jnp.concatenate(stack, axis=0).T
        return column, jnp.log2(dt) - c2

    def prepare_some(step, carry):
        base = pl.multiple_of(step * together * TILE, TILE)
        rows = pl.ds(base, together * TILE)
        made = [prepare(step * together + n) for n in range(together)]
        narrow = jnp.concatenate([column for column, _ in made], axis=0).astype(BF16)
        wide = dot(narrow, re[1])
        grown = dot(narrow, re[0])
        scaled = (rx[rows, :].astype(F32) * wide).astype(BF16)
        rgrown[rows, :] = grown
        rv[pl.ds(step * together + 2, together)] = scaled.reshape(together, TILE, cb)
        for n, (column, row_form) in enumerate(made):
            tile = step * together + n
            rt[tile] = column
            rrow[tile] = row_form
            rtot[tile + 2] = jnp.broadcast_to(grown[(n + 1) * TILE - 1 : (n + 1) * TILE], (8, cb))
        return carry

    def within(tile):
        base = pl.multiple_of(tile * TILE, TILE)
        rows = pl.ds(base, TILE)
        column = rt[tile]
        x_tile = rx[rows, :]
        grown = rgrown[rows, :]
        c_rows = rbc[pl.ds(base + 2 * TILE, TILE), STATE:]
        scores = dot_nt(c_rows, rbc[pl.ds(base, 3 * TILE), :STATE])
        j = iota((TILE, 3 * TILE), 1) - 2 * TILE
        first = column[:, 7 * head_rows : 7 * head_rows + 1].astype(jnp.int32)
        seen = (j <= iota((TILE, 3 * TILE), 0)) & (j >= first)
        bias = jnp.where(seen[:, 2 * TILE :], 0.0, -1e30)
        cross = jnp.where(seen[:, : 2 * TILE], scores[:, : 2 * TILE], 0.0).astype(BF16)
        earlier = dot(cross[:, TILE:], rv[tile + 1]) + rtot[tile + 1, 0:1] * dot(cross[:, :TILE], rv[tile])
        pieces = diagonal(column, rrow[tile], bias, scores[:, 2 * TILE :], x_tile, block_heads)
        skip = dwide[0:1, my_cols]
        return jnp.concatenate(pieces, axis=1) + grown * earlier + skip * x_tile.astype(F32)

    def response_tiles(step, carry):
        places = [step * 4 + n for n in range(4)]
        made = [within(tile) for tile in places]
        for tile, total in zip(places, made):
            racc[pl.ds(pl.multiple_of(tile * TILE, TILE), TILE), :] = total
        return carry

    def relay(distance):
        @pl.when(z >= distance)
        def _():
            seed_copy(z - distance, twin, tu_send.at[distance]).wait_recv()
            pass_on(z - distance, distance, True)
            seed_copy(z - distance, twin, tu_send.at[distance]).start()

        @pl.when(z + distance < levels)
        def _():
            seed_copy(z + distance, twin, td_send.at[distance]).wait_recv()
            pass_on(z + distance, distance, False)
            seed_copy(z + distance, twin, td_send.at[distance]).start()

    together = 8
    share = tiles // 16
    lax.fori_loop(0, tiles // together, prepare_some, 0)
    relay(1)
    lax.fori_loop(0, share, response_tiles, 0)
    for distance in range(2, levels):
        relay(distance)
        if distance < 4:
            lax.fori_loop((distance - 1) * share, distance * share, response_tiles, 0)
    lax.fori_loop((min(levels, 4) - 1) * share, 4 * share, response_tiles, 0)

    for step in range(1, seqs):
        copy = prefix_copy(step)[1]

        @pl.when(me > 0)
        def _():
            copy.wait_recv()

    @pl.when(me == 0)
    def _():
        for s in range(seqs):
            precv[s] = jnp.zeros((STATE, cb), BF16)

    narrow = jnp.concatenate([pt[0], pt[2]], axis=0).astype(BF16)
    later = iota((2 * TILE, cb), 0) >= TILE
    for s in range(seqs):
        here = slice(s * cb, (s + 1) * cb)
        grown = dot(narrow, pe[0, :, here]) * jnp.where(later, ptot[0, 0:1, here], 1.0)
        carried = grown * dot(pbc[:, STATE:], precv[s])
        pout[:, here] = (pacc[:, here] + carried).astype(BF16)
    p_outs = [pltpu.make_async_copy(pout, pout_hbm, out_sem.at[tiles])]
    p_outs[0].start()

    for level in range(levels):
        which = level * 2 + 1 - core
        pltpu.make_async_remote_copy(
            src_ref=seeds.at[which], dst_ref=seeds.at[which], send_sem=tu_send.at[0], recv_sem=g_recv.at[which],
            device_id={"grp": twin}, device_id_type=MESH).wait_recv()

    def out_copy(step):
        rows = pl.ds(pl.multiple_of(step * together * TILE, TILE), together * TILE)
        return pltpu.make_async_copy(rout.at[rows], rout_hbm.at[rows], out_sem.at[step])

    def seed_tiles(step, carry):
        base = pl.multiple_of(step * together * TILE, TILE)
        rows = pl.ds(base, together * TILE)
        column = rt[pl.ds(step * together, together)].reshape(together * TILE, TILE)
        owner = column[:, 7 * head_rows + 1 : 7 * head_rows + 2].astype(jnp.int32)
        c_rows = rbc[pl.ds(base + 2 * TILE, together * TILE), STATE:].astype(F32)
        batch = 8 if grps % 8 == 0 else 2
        total = jnp.zeros((together * TILE, cb), F32)
        for q in range(0, grps, batch):
            chosen = [jnp.where(owner == q + n, c_rows, 0.0).astype(BF16) for n in range(batch)]
            table = seeds[q : q + batch].reshape(batch * STATE, cb)
            total = total + dot(jnp.concatenate(chosen, axis=1), table)
        result = racc[rows, :] + dot(column.astype(BF16), re[2]) * total
        rout[rows, :] = jnp.where(owner >= 0, result, 0.0).astype(BF16)
        out_copy(step).start()
        return carry

    lax.fori_loop(0, tiles // together, seed_tiles, 0)

    for step in range(1, seqs):
        state_copy(step).wait_send()
        peer, copy = prefix_copy(step)

        @pl.when(peer > 0)
        def _():
            copy.wait_send()

    for distance in range(levels):
        @pl.when((z >= distance) & (z < levels - 1))
        def _():
            seed_copy(z - distance, g + 2, up_send.at[distance]).wait_send()

        @pl.when((z + distance < levels) & (z > 0))
        def _():
            seed_copy(z + distance, g - 2, down_send.at[distance]).wait_send()

        @pl.when(z >= distance)
        def _():
            seed_copy(z - distance, twin, tu_send.at[distance]).wait_send()

        if distance > 0:
            @pl.when(z + distance < levels)
            def _():
                seed_copy(z + distance, twin, td_send.at[distance]).wait_send()

    for copy in p_outs:
        copy.wait()

    def out_wait(step, carry):
        out_copy(step).wait()
        return carry

    lax.fori_loop(0, tiles // together, out_wait, 0)


def on_device(
    p_x, p_bc, p_dt, p_decay, r_x, r_bc, r_dt, r_decay, pack_list, resp_len, resp_prompt, d_skip
):
    seqs, grps = lax.axis_size("seq"), lax.axis_size("grp")
    heads = p_dt.shape[1]
    block_heads = heads // seqs
    head_rows = max(8, block_heads)
    slots = pack_list.shape[1]
    tiles = r_x.shape[0] // TILE
    cols, cb = heads * CHANNELS, block_heads * CHANNELS
    if head_rows > block_heads:
        extra = ((0, head_rows - block_heads), (0, 0))
        r_dt, r_decay = jnp.pad(r_dt, extra, constant_values=1.0), jnp.pad(r_decay, extra)
    sizes = (seqs, grps, heads, block_heads, head_rows, slots, tiles)
    levels = grps // 2
    anywhere = pl.BlockSpec(memory_space=pl.ANY)
    dma = pltpu.SemaphoreType.DMA
    p_out, r_out = pl.pallas_call(
        functools.partial(kernel, sizes),
        out_shape=(
            jax.ShapeDtypeStruct((2 * TILE, cols), BF16),
            jax.ShapeDtypeStruct((tiles * TILE, cb), BF16),
        ),
        in_specs=[pl.BlockSpec(memory_space=pltpu.HBM)] * 12,
        out_specs=(anywhere, anywhere),
        scratch_shapes=[
            pltpu.VMEM(p_dt.shape[1:], F32),
            pltpu.VMEM(p_decay.shape[1:], F32),
            pltpu.VMEM(r_dt.shape, F32),
            pltpu.VMEM(r_decay.shape, F32),
            pltpu.SMEM(pack_list.shape, jnp.int32),
            pltpu.SMEM(resp_len.shape, jnp.int32),
            pltpu.SMEM(resp_prompt.shape, jnp.int32),
            pltpu.VMEM((1, heads), F32),
            pltpu.VMEM((tiles, head_rows, TILE), F32),
            pltpu.VMEM((tiles * TILE, cb), F32),
            pltpu.VMEM((2 * TILE, cols), BF16),
            pltpu.VMEM((2 * TILE, 2 * STATE), BF16),
            pltpu.VMEM((tiles * TILE, cb), BF16),
            pltpu.VMEM(((tiles + 2) * TILE, 2 * STATE), BF16),
            pltpu.VMEM((2, TILE, cols), BF16),
            pltpu.VMEM((4, TILE, TILE), F32),
            pltpu.VMEM((2, TILE, cols), BF16),
            pltpu.VMEM((2, 8, cols), F32),
            pltpu.VMEM((2 * TILE, cols), F32),
            pltpu.VMEM((8, cols), F32),
            pltpu.VMEM((tiles + 2, TILE, cb), BF16),
            pltpu.VMEM((tiles, TILE, TILE), F32),
            pltpu.VMEM((3, TILE, cb), BF16),
            pltpu.VMEM((tiles + 2, 8, cb), F32),
            pltpu.VMEM((tiles * TILE, cb), F32),
            pltpu.VMEM((4 * head_rows, (tiles + 2) * TILE), BF16),
            pltpu.VMEM((seqs, STATE + 16, cb), BF16),
            pltpu.VMEM((seqs, STATE + 16, cb), BF16),
            pltpu.VMEM((seqs, STATE, cb), BF16),
            pltpu.VMEM((seqs, STATE, cb), BF16),
            pltpu.VMEM((grps, STATE, cb), BF16),
            pltpu.VMEM((2 * TILE, cols), BF16),
            pltpu.VMEM((tiles * TILE, cb), BF16),
            dma((12,)),
            dma((tiles + 2,)),
            dma((seqs,)),
            dma((seqs,)),
            dma((seqs,)),
            dma((seqs,)),
            dma((grps,)),
            dma((levels,)),
            dma((levels,)),
            dma((levels,)),
            dma((levels,)),
        ],
        compiler_params=pltpu.CompilerParams(
            collective_id=0, has_side_effects=True, vmem_limit_bytes=63 * 2**20
        ),
        cost_estimate=pl.CostEstimate(flops=4 * 10**9, bytes_accessed=8 * 10**6, transcendentals=4 * 10**6),
        name="scan_and_seeds",
    )(
        p_x[0], p_bc[0], p_dt[0], p_decay[0], r_x, r_bc, r_dt, r_decay,
        pack_list, resp_len, resp_prompt, d_skip[None],
    )
    return p_out[None], r_out


def solution(mesh):
    placed = (
        P("grp", "seq", None),
        P("grp", "seq", None),
        P("grp", None, "seq"),
        P("grp", None, "seq"),
        P("grp", "seq"),
        P("grp", None),
        P("seq", "grp"),
        P("seq", "grp"),
        P("grp", None),
        P(),
        P(),
        P(),
    )
    return jax.shard_map(
        on_device,
        mesh=mesh,
        in_specs=placed,
        out_specs=(P("grp", "seq", None), P("grp", "seq")),
        check_vma=False,
    )
```
